128 devices in a mesh: fsdp: 16 (over z, y), rep: 8 (over x, core).
Axes of the slice: x: 4, y: 4, z: 4, core: 2. Of those that a mesh axis runs over, the one named last changes fastest.
Arguments:
- gradient: bfloat16 [8192, 4096], P('fsdp', 'rep'), may hold values from -0.1875 to 0.1875
- first_moment: float32 [8192, 4096], P('fsdp', 'rep'), may hold values from -0.1875 to 0.1875
- second_moment: float32 [8192, 4096], P('fsdp', 'rep'), may hold values from 0.0001 to 0.004
- factors: float32 [256, 1024, 1024], P(('fsdp', 'rep')), may hold values from -0.125 to 0.125
- eigen_bases: bfloat16 [256, 1024, 1024], P(('fsdp', 'rep')), may hold values from -0.1875 to 0.1875
- owners: int32 [64], replicated, may hold values from 0 to 127, as said below
Outputs:
- update: float32 [8192, 4096], P('fsdp', 'rep')
- new_first: float32 [8192, 4096], P('fsdp', 'rep')
- new_second: float32 [8192, 4096], P('fsdp', 'rep')
- new_factors: float32 [256, 1024, 1024], P(('fsdp', 'rep'))
The draws below stay inside these ranges and needn't reach their ends.
Inputs may be any that keep to these rules, and one draw needn't show every extreme that they name: `owners`: no device is named by more than 2 items, and in every draw some devices are named by exactly 2.
All inputs are finite; a program needn't handle non-finite values.
Results may differ from the reference program's by a relative error of at most 0.0041.
Values may be sent and summed in bfloat16 or wider, within the bound.
No kernel may reach another device: no remote copies, remote signals or barrier semaphores. Data moves between devices by JAX's collectives and lax.ppermute only.
A program may use at most 128 MiB of HBM per device.

```python
import math
import jax
import jax.numpy as jnp
from jax import lax

BS = 1024
SLOTS = 2
ROWS = 8192
COLS = 4096
ITEMS = 64
N_FSDP = 16
N_REP = 8


def draw_owners(key, part):
    key = jax.random.fold_in(key, 11)
    order_key, head_key, shuffle_key = jax.random.split(key, 3)
    devices = N_FSDP * N_REP
    heavy_count = ITEMS // 4
    used_count = ITEMS - heavy_count
    middle = jax.random.permutation(order_key, devices - 2).astype(jnp.int32) + 1
    ends = jnp.array([devices - 1, 0], dtype=jnp.int32)
    device_list = jnp.concatenate([ends, middle], axis=0)[:used_count]
    device_order = device_list[jax.random.permutation(head_key, used_count)]
    positions = jnp.arange(ITEMS, dtype=jnp.int32)
    device_pick = jnp.where(positions < 2 * heavy_count, positions // 2, positions - heavy_count)
    assigned = device_order[device_pick]
    shuffle = jax.random.permutation(shuffle_key, ITEMS)
    return assigned[shuffle].astype(jnp.int32)


def steps_of(stream_key, dims, cuts, low, top_value):
    loudness, own = 1.0, jax.random.fold_in(stream_key, 6)
    for dim, blocks in cuts:
        heights = jnp.exp(jax.random.uniform(jax.random.fold_in(own, dim), (blocks,), jnp.float32, low / len(cuts), top_value / len(cuts)))
        loudness = loudness * jnp.repeat(heights, dims[dim] // blocks).reshape([-1 if axis == dim else 1 for axis in range(len(dims))])
    return loudness


def scatter_about(rng, extent, spread, reach, shards=(), held_as=jnp.bfloat16):
    result = jax.random.normal(rng, extent, jnp.float32) * spread
    if len(shards) > 0:
        result = steps_of(rng, extent, shards, -0.22, 0.18) * result
    return jnp.clip(result, min=-reach, max=reach).astype(held_as)


def setup_inputs(seed: int = 0) -> dict:
    key_list = jax.random.split(jax.random.key(seed), 7)
    gradient = scatter_about(key_list[0], (ROWS, COLS), 0.03125, 0.1875, ((0, 16), (1, 8)))
    first_moment = scatter_about(key_list[1], (ROWS, COLS), 0.03125, 0.1875, ((0, 16), (1, 8)), jnp.float32)
    second_moment = jnp.clip(jnp.exp(math.log(0.004) - 3.6888795 * jax.random.uniform(key_list[2], (ROWS, COLS), jnp.float32) ** steps_of(key_list[2], (ROWS, COLS), ((0, 16), (1, 8)), -0.2, 0.2)), 0.0001, 0.004)
    factors = scatter_about(key_list[3], (N_FSDP * N_REP * SLOTS, BS, BS), 0.02, 0.125, ((0, 128),), jnp.float32)
    eigen_bases = scatter_about(key_list[4], (N_FSDP * N_REP * SLOTS, BS, BS), BS ** -0.5, 0.1875, ((0, 128),))
    owners = draw_owners(jax.random.fold_in(key_list[6], 71), 0)
    return dict(gradient=gradient, first_moment=first_moment, second_moment=second_moment, factors=factors, eigen_bases=eigen_bases, owners=owners)


beta_one = 0.9
beta_two = 0.95
shampoo_beta = 0.95
epsilon = 1e-08

def product_tn(left, right):
    return lax.dot_general(left, right, (((0,), (0,)), ((), ())), preferred_element_type=jnp.float32)

def product_nt(left, right):
    return lax.dot_general(left, right, (((1,), (1,)), ((), ())), preferred_element_type=jnp.float32)

def reference(gradient, first_moment, second_moment, factors, eigen_bases, owners):
    block_cols = COLS // BS
    block_rows = ROWS // BS
    item_count = owners.shape[0]
    item_index = jnp.arange(item_count, dtype=jnp.int32)
    earlier_same = (owners[:, None] == owners[None, :]) & (item_index[None, :] < item_index[:, None])
    slot_codes = (SLOTS * owners + lax.optimization_barrier(jnp.sum(earlier_same.astype(jnp.int32), axis=1))).astype(jnp.int32)
    update_grid = []
    first_grid = []
    second_grid = []
    grams = []
    for block_row in range(block_rows):
        update_line = []
        first_line = []
        second_line = []
        for block_col in range(block_cols):
            block_id = block_row * block_cols + block_col
            row_lo = block_row * BS
            col_lo = block_col * BS
            grad_block = gradient[row_lo:row_lo + BS, col_lo:col_lo + BS]
            left_basis = eigen_bases[slot_codes[2 * block_id]]
            right_basis = eigen_bases[slot_codes[2 * block_id + 1]]
            left_rot = product_tn(left_basis, grad_block).astype(jnp.bfloat16)
            rotated = jnp.dot(left_rot, right_basis, preferred_element_type=jnp.float32)
            first_block = beta_one * first_moment[row_lo:row_lo + BS, col_lo:col_lo + BS] + (1.0 - beta_one) * rotated
            second_block = beta_two * second_moment[row_lo:row_lo + BS, col_lo:col_lo + BS] + (1.0 - beta_two) * rotated * rotated
            direction = (first_block / (jnp.sqrt(second_block) + epsilon)).astype(jnp.bfloat16)
            back_left = jnp.dot(left_basis, direction, preferred_element_type=jnp.float32).astype(jnp.bfloat16)
            update_line.append(product_nt(back_left, right_basis))
            first_line.append(first_block)
            second_line.append(second_block)
            grams.append(product_nt(grad_block, grad_block))
            grams.append(product_tn(grad_block, grad_block))
        update_grid.append(update_line)
        first_grid.append(first_line)
        second_grid.append(second_line)
    gram_stack = jnp.stack(grams, axis=0)
    gram_full = jnp.zeros_like(factors).at[slot_codes].set(gram_stack)
    present = jnp.zeros((factors.shape[0],), jnp.float32).at[slot_codes].set(1.0)
    new_factors = jnp.where(present[:, None, None] > 0.5, shampoo_beta * factors + (1.0 - shampoo_beta) * gram_full, factors)
    return (jnp.block(update_grid), jnp.block(first_grid), jnp.block(second_grid), new_factors)
```

```python
import functools

import jax
import jax.numpy as jnp
from jax import lax
from jax.experimental import pallas as pl
from jax.experimental.pallas import tpu as pltpu
from jax.sharding import PartitionSpec as P

beta_one = 0.9
beta_two = 0.95
shampoo_beta = 0.95
epsilon = 1e-08

SUB = 8
GB = 256
PAIRS = (
    ((0, 0), (0, 1), (0, 2), (0, 3), (1, 1)),
    ((1, 2), (1, 3), (2, 2), (2, 3), (3, 3)),
)
BOTH = ("fsdp", "rep")
PARAMS = pltpu.CompilerParams(vmem_limit_bytes=56 * 2**20)


def swap_neighbour(value, axis):
    pairs = [(source, source ^ 1) for source in range(lax.axis_size(axis))]
    return lax.ppermute(value, axis, pairs)


def dot_nn(left, right):
    return jnp.dot(left, right, preferred_element_type=jnp.float32)


def dot_tn(left, right):
    return lax.dot_general(
        left, right, (((0,), (0,)), ((), ())), preferred_element_type=jnp.float32
    )


def dot_nt(left, right):
    return lax.dot_general(
        left, right, (((1,), (1,)), ((), ())), preferred_element_type=jnp.float32
    )


def whole(memory_space=pltpu.VMEM):
    return pl.BlockSpec(memory_space=memory_space)


def interleave_kernel(src_ref, dst_ref):
    dst_ref[:, 0] = src_ref[0]


def interleave(bases, devices):
    slots, size, _ = bases.shape
    parts = bases.reshape(slots, devices, SUB, size)
    step = devices // 4
    return pl.pallas_call(
        interleave_kernel,
        grid=(4, slots),
        in_specs=[pl.BlockSpec((1, step, SUB, size), lambda p, s: (s, p, 0, 0))],
        out_specs=pl.BlockSpec((step, 1, SUB, size), lambda p, s: (p, s, 0, 0)),
        out_shape=jax.ShapeDtypeStruct((devices, slots, SUB, size), bases.dtype),
        compiler_params=PARAMS,
        name="interleave",
    )(parts)


def place_quads(row, col, quads, block_ref):
    half = quads[0].shape[0]
    for dr in range(2):
        for dc in range(2):
            at = (pl.multiple_of((row ^ dr) * half, half), pl.multiple_of((col ^ dc) * half, half))
            block_ref[pl.ds(at[0], half), pl.ds(at[1], half)] = quads[2 * dr + dc][...]


def gram_kernel(place_ref, own_ref, side_ref, below_ref, cross_ref, out_ref, block_ref):
    row = place_ref[0]
    col = place_ref[1]
    place_quads(row, col, (own_ref, side_ref, below_ref, cross_ref), block_ref)

    def emit(left_gram, which):
        for n, (first, second) in enumerate(PAIRS[which]):
            a = slice(first * GB, (first + 1) * GB)
            b = slice(second * GB, (second + 1) * GB)
            if left_gram:
                value = dot_nt(block_ref[a, :], block_ref[b, :])
            else:
                value = dot_tn(block_ref[:, a], block_ref[:, b])
            for half in range(2):
                tiles = value[:, half * 128 : (half + 1) * 128].reshape(GB // 8, 8, 128)
                tiles = tiles.astype(jnp.bfloat16)
                for r in (n // 2,) if n < 4 else (0, 1):
                    t = n % 2 if n < 4 else 2
                    out_ref[:, 2 * half + r, :, t * 128 : (t + 1) * 128] = tiles

    for left_gram in (True, False):
        for which in range(2):
            pl.when((col == (0 if left_gram else 1)) & (row == which))(
                functools.partial(emit, left_gram, which)
            )


def gram_pieces(place, quads):
    size = 2 * quads[0].shape[0]
    return pl.pallas_call(
        gram_kernel,
        in_specs=[whole(pltpu.SMEM)] + [whole()] * 4,
        out_specs=whole(),
        out_shape=jax.ShapeDtypeStruct((32, 4, 8, 384), jnp.bfloat16),
        scratch_shapes=[pltpu.VMEM((size, size), jnp.bfloat16)],
        compiler_params=PARAMS,
        cost_estimate=pl.CostEstimate(flops=7 * 10**8, bytes_accessed=3 * 10**6, transcendentals=0),
        name="gram_pieces",
    )(place, *quads)


def second_kernel(codes_ref, rows_ref, gram_ref, out_ref):
    out_ref[:, :, 768:] = gram_ref[...]

    @pl.loop(0, 32)
    def _(block):
        left = rows_ref[codes_ref[2 * block]]
        right = rows_ref[codes_ref[2 * block + 1]]
        base = (block // 4) * 16 + (block % 4) * 2
        for i in range(2):
            at = base + 8 * i
            out_ref[at, :, 0:512] = left[:, 512 * i : 512 * (i + 1)]
            out_ref[at, :, 512:768] = right[:, 0:256]
            out_ref[at + 1, :, 0:768] = right[:, 256:1024]


def second_operand(codes, rows, gram):
    return pl.pallas_call(
        second_kernel,
        in_specs=[whole(pltpu.SMEM), whole(), whole()],
        out_specs=whole(),
        out_shape=jax.ShapeDtypeStruct((128, SUB, 1152), jnp.bfloat16),
        compiler_params=PARAMS,
        cost_estimate=pl.CostEstimate(flops=0, bytes_accessed=8 * 10**6, transcendentals=0),
        name="second_operand",
    )(codes, rows, gram)


def third_kernel(codes_ref, place_ref, got_ref, out_ref):
    core = place_ref[1]

    @pl.loop(0, 64)
    def _(item):
        block = item // 2
        at = codes_ref[item]
        upper = (block // 4) * 16 + (block % 4) * 2 + item % 2
        lower = upper + 8
        out_ref[at, :, 0:256] = got_ref[upper, :, 0:256]
        out_ref[at, :, 256:512] = got_ref[lower, :, 0:256]
        out_ref[at, :, 512:640] = got_ref[upper + 8 * core, :, 256:384]


def third_operand(codes, place, got):
    return pl.pallas_call(
        third_kernel,
        grid=(1,),
        in_specs=[
            whole(pltpu.SMEM),
            whole(pltpu.SMEM),
            pl.BlockSpec((128, SUB, 384), lambda _: (0, 0, 2)),
        ],
        out_specs=pl.BlockSpec((256, SUB, 640), lambda _: (0, 0, 0)),
        out_shape=jax.ShapeDtypeStruct((256, SUB, 640), jnp.bfloat16),
        compiler_params=PARAMS,
        cost_estimate=pl.CostEstimate(flops=0, bytes_accessed=4 * 10**6, transcendentals=0),
        name="third_operand",
    )(codes, place, got)


def rotate_kernel(
    place_ref,
    own_ref,
    side_ref,
    below_ref,
    cross_ref,
    mine_ref,
    theirs_ref,
    first_ref,
    second_ref,
    new_first_ref,
    new_second_ref,
    direction_ref,
    block_ref,
    left_ref,
    right_ref,
):
    row = place_ref[0]
    col = place_ref[1]
    place_quads(row, col, (own_ref, side_ref, below_ref, cross_ref), block_ref)

    @pl.when(col == 0)
    def _():
        left_ref[...] = mine_ref[:, :, 0:512]
        right_ref[:, :, 0:256] = mine_ref[:, :, 512:768]
        right_ref[:, :, 256:512] = theirs_ref[:, :, 0:256]

    @pl.when(col == 1)
    def _():
        left_ref[...] = theirs_ref[:, :, 0:512]
        right_ref[...] = mine_ref[:, :, 256:768]

    left = left_ref[...].reshape(1024, 512)
    left_rot = dot_tn(left, block_ref[...]).astype(jnp.bfloat16)
    rotated = dot_nn(left_rot, right_ref[...].reshape(1024, 512))
    new_first = beta_one * first_ref[...] + (1.0 - beta_one) * rotated
    new_second = beta_two * second_ref[...] + (1.0 - beta_two) * rotated * rotated
    new_first_ref[...] = new_first
    new_second_ref[...] = new_second
    direction_ref[...] = (new_first / (jnp.sqrt(new_second) + epsilon)).astype(jnp.bfloat16)


def rotate(place, quads, mine, theirs, first, second):
    half = first.shape[0]
    return pl.pallas_call(
        rotate_kernel,
        grid=(1,),
        in_specs=[whole(pltpu.SMEM)]
        + [pl.BlockSpec((half, half), lambda _: (0, 0))] * 4
        + [pl.BlockSpec((128, SUB, 768), lambda _: (0, 0, 0))] * 2
        + [pl.BlockSpec((half, half), lambda _: (0, 0))] * 2,
        out_specs=[pl.BlockSpec((half, half), lambda _: (0, 0))] * 3,
        out_shape=[
            jax.ShapeDtypeStruct((half, half), jnp.float32),
            jax.ShapeDtypeStruct((half, half), jnp.float32),
            jax.ShapeDtypeStruct((half, half), jnp.bfloat16),
        ],
        scratch_shapes=[
            pltpu.VMEM((1024, 1024), jnp.bfloat16),
            pltpu.VMEM((128, SUB, 512), jnp.bfloat16),
            pltpu.VMEM((128, SUB, 512), jnp.bfloat16),
        ],
        compiler_params=PARAMS,
        cost_estimate=pl.CostEstimate(
            flops=16 * 10**8, bytes_accessed=10**7, transcendentals=10**6
        ),
        name="rotate",
    )(place, *quads, mine, theirs, first, second)


def back_kernel(
    place_ref,
    own_ref,
    side_ref,
    mine_ref,
    theirs_ref,
    keep_ref,
    give_ref,
    left_ref,
    right_ref,
    strip_ref,
):
    row = place_ref[0]
    col = place_ref[1]
    half = own_ref.shape[0]
    strip_ref[:, pl.ds(pl.multiple_of(col * half, half), half)] = own_ref[...]
    strip_ref[:, pl.ds(pl.multiple_of((1 - col) * half, half), half)] = side_ref[...]

    @pl.when(col == 0)
    def _():
        left_ref[...] = mine_ref[:, :, 0:512]
        right_ref[:, :, 0:256] = mine_ref[0:64, :, 512:768]
        right_ref[:, :, 256:1024] = theirs_ref[0:64]

    @pl.when(col == 1)
    def _():
        left_ref[...] = theirs_ref[:, :, 0:512]
        right_ref[:, :, 0:256] = theirs_ref[64:128, :, 512:768]
        right_ref[:, :, 256:1024] = mine_ref[64:128]

    half_back = dot_nt(strip_ref[...], right_ref[...].reshape(512, 1024)).astype(jnp.bfloat16)
    groups = half // SUB
    keep = left_ref[pl.ds(row * groups, groups)].reshape(half, 512)
    give = left_ref[pl.ds((1 - row) * groups, groups)].reshape(half, 512)
    keep_ref[...] = dot_nn(keep, half_back)
    give_ref[...] = dot_nn(give, half_back).astype(jnp.bfloat16)


def back(place, own, side, mine, theirs):
    half = own.shape[0]
    return pl.pallas_call(
        back_kernel,
        grid=(1,),
        in_specs=[whole(pltpu.SMEM)]
        + [pl.BlockSpec((half, half), lambda _: (0, 0))] * 2
        + [pl.BlockSpec((128, SUB, 768), lambda _: (0, 0, 0))] * 2,
        out_specs=[pl.BlockSpec((half, half), lambda _: (0, 0))] * 2,
        out_shape=[
            jax.ShapeDtypeStruct((half, half), jnp.float32),
            jax.ShapeDtypeStruct((half, half), jnp.bfloat16),
        ],
        scratch_shapes=[
            pltpu.VMEM((128, SUB, 512), jnp.bfloat16),
            pltpu.VMEM((64, SUB, 1024), jnp.bfloat16),
            pltpu.VMEM((half, 2 * half), jnp.bfloat16),
        ],
        compiler_params=PARAMS,
        cost_estimate=pl.CostEstimate(flops=11 * 10**8, bytes_accessed=6 * 10**6, transcendentals=0),
        name="back",
    )(place, own, side, mine, theirs)


def factor_kernel(live_ref, factor_ref, got_ref, out_ref):
    slot = pl.program_id(0)
    strip = pl.program_id(1)
    live = live_ref[slot] != 0

    def piece(first, second):
        which, n = next(
            (w, n) for w in range(2) for n in range(5) if PAIRS[w][n] == (first, second)
        )
        r = n // 2 if n < 4 else which
        lane = 2 * which + n % 2 if n < 4 else 4
        halves = [
            got_ref[:, 2 * h + r, slot, :, lane * 128 : (lane + 1) * 128]
            .astype(jnp.float32)
            .reshape(GB, 128)
            for h in range(2)
        ]
        return jnp.concatenate(halves, axis=1)

    def mix(row):
        for col in range(4):
            value = piece(row, col) if row <= col else piece(col, row).T
            at = slice(col * GB, (col + 1) * GB)
            out_ref[0, :, at] = (
                shampoo_beta * factor_ref[0, :, at] + (1.0 - shampoo_beta) * value
            )

    for row in range(4):
        pl.when(live & (strip == row))(functools.partial(mix, row))

    @pl.when(jnp.logical_not(live))
    def _():
        out_ref[...] = factor_ref[...]


def update_factors(live, factors, got):
    slots, size, _ = factors.shape
    got = got.reshape(32, 4, slots, SUB, 640)
    return pl.pallas_call(
        factor_kernel,
        grid=(slots, 4),
        in_specs=[
            whole(pltpu.SMEM),
            pl.BlockSpec((1, GB, size), lambda s, p: (s, p, 0)),
            whole(),
        ],
        out_specs=pl.BlockSpec((1, GB, size), lambda s, p: (s, p, 0)),
        out_shape=jax.ShapeDtypeStruct(factors.shape, factors.dtype),
        compiler_params=PARAMS,
        cost_estimate=pl.CostEstimate(
            flops=4 * 10**6, bytes_accessed=2 * 10**7, transcendentals=0
        ),
        name="update_factors",
    )(live, factors, got)


def shards(gradient, first_moment, second_moment, factors, eigen_bases, owners):
    devices = lax.axis_size("fsdp") * lax.axis_size("rep")
    slots = factors.shape[0]
    size = factors.shape[1]
    item_count = owners.shape[0]
    fsdp_index = lax.axis_index("fsdp")
    rep_index = lax.axis_index("rep")
    my_index = fsdp_index * lax.axis_size("rep") + rep_index
    place = jnp.stack([fsdp_index % 2, rep_index % 2]).astype(jnp.int32)

    first_parts = interleave(eigen_bases, devices)
    first_got = lax.all_to_all(first_parts, BOTH, 0, 0, tiled=True)

    item_index = jnp.arange(item_count, dtype=jnp.int32)
    earlier_same = (owners[:, None] == owners[None, :]) & (
        item_index[None, :] < item_index[:, None]
    )
    codes = slots * owners + jnp.sum(earlier_same.astype(jnp.int32), axis=1)
    my_codes = my_index * slots + jnp.arange(slots, dtype=jnp.int32)
    live = jnp.sum((codes[None, :] == my_codes[:, None]).astype(jnp.int32), axis=1)

    side = swap_neighbour(gradient, "rep")
    below = swap_neighbour(gradient, "fsdp")
    cross = swap_neighbour(below, "rep")
    quads = (gradient, side, below, cross)
    gram = gram_pieces(place, quads).reshape(devices, SUB, 384)

    second_parts = second_operand(codes, first_got.reshape(devices * slots, SUB, size), gram)
    mine = lax.all_to_all(second_parts, BOTH, 0, 0, tiled=True)
    theirs = swap_neighbour(mine[:, :, :768], "rep")

    third_parts = third_operand(codes, place, mine).reshape(devices, slots, SUB, 640)
    third_got = lax.all_to_all(third_parts, BOTH, 0, 0, tiled=True)

    new_first, new_second, direction = rotate(
        place, quads, mine, theirs, first_moment, second_moment
    )
    other = swap_neighbour(direction, "rep")
    keep, give = back(place, direction, other, mine, theirs)
    update = keep + swap_neighbour(give, "fsdp").astype(jnp.float32)
    new_factors = update_factors(live, factors, third_got)
    return (update, new_first, new_second, new_factors)


def solution(mesh):
    in_specs = (
        P("fsdp", "rep"),
        P("fsdp", "rep"),
        P("fsdp", "rep"),
        P(("fsdp", "rep"), None, None),
        P(("fsdp", "rep"), None, None),
        P(),
    )
    out_specs = (
        P("fsdp", "rep"),
        P("fsdp", "rep"),
        P("fsdp", "rep"),
        P(("fsdp", "rep"), None, None),
    )
    return jax.shard_map(shards, mesh=mesh, in_specs=in_specs, out_specs=out_specs, check_vma=False)
```

```python
import functools

import jax
import jax.numpy as jnp
from jax import lax
from jax.experimental import pallas as pl
from jax.experimental.pallas import tpu as pltpu
from jax.sharding import PartitionSpec as P

beta_one = 0.9
beta_two = 0.95
shampoo_beta = 0.95
epsilon = 1e-08

SUB = 8
GB = 256
ABOVE = (((0, 1), (0, 2), (0, 3)), ((1, 2), (1, 3), (2, 3)))
WIDTH = 2 * 128
BOTH = ("fsdp", "rep")
PARAMS = pltpu.CompilerParams(vmem_limit_bytes=24 * 2**20)


def swap_neighbour(value, axis):
    pairs = [(source, source ^ 1) for source in range(lax.axis_size(axis))]
    return lax.ppermute(value, axis, pairs)


def dot_nn(left, right):
    return jnp.dot(left, right, preferred_element_type=jnp.float32)


def dot_tn(left, right):
    return lax.dot_general(
        left, right, (((0,), (0,)), ((), ())), preferred_element_type=jnp.float32
    )


def dot_nt(left, right):
    return lax.dot_general(
        left, right, (((1,), (1,)), ((), ())), preferred_element_type=jnp.float32
    )


def whole(memory_space=pltpu.VMEM):
    return pl.BlockSpec(memory_space=memory_space)


def interleave_kernel(src_ref, dst_ref, held_ref, sems):
    slots, devices = held_ref.shape[0], held_ref.shape[1]
    stores = []
    loads = []
    for n in range(2 * slots):
        slot, span = n % slots, pl.ds(n // slots * (devices // 2), devices // 2)
        held = held_ref.at[slot, span]
        loads.append(pltpu.make_async_copy(src_ref.at[slot, span], held, sems.at[0, n]))
        stores.append(pltpu.make_async_copy(held, dst_ref.at[span, slot], sems.at[1, n]))
        loads[n].start()
    for load, store in zip(loads, stores):
        load.wait()
        store.start()
    for store in stores:
        store.wait()


def interleave(bases, devices):
    slots, size, _ = bases.shape
    parts = bases.reshape(slots, devices, SUB, size)
    return pl.pallas_call(
        interleave_kernel,
        in_specs=[whole(pl.ANY)],
        out_specs=whole(pl.ANY),
        out_shape=pltpu.HBM((devices, slots, SUB, size), bases.dtype),
        scratch_shapes=[
            pltpu.VMEM(parts.shape, bases.dtype),
            pltpu.SemaphoreType.DMA((2, 2 * slots)),
        ],
        compiler_params=pltpu.CompilerParams(vmem_limit_bytes=8 * 2**20),
        cost_estimate=pl.CostEstimate(flops=0, bytes_accessed=8 * 10**6, transcendentals=0),
        name="interleave",
    )(pltpu.with_memory_space_constraint(parts, pltpu.HBM))


def place_quads(row, col, quads, block_ref):
    half = quads[0].shape[0]
    for dr in range(2):
        for dc in range(2):
            at = (pl.multiple_of((row ^ dr) * half, half), pl.multiple_of((col ^ dc) * half, half))
            block_ref[pl.ds(at[0], half), pl.ds(at[1], half)] = quads[2 * dr + dc][...]


def grid_positions():
    shape = (GB, GB)
    return lax.broadcasted_iota(jnp.int32, shape, 0), lax.broadcasted_iota(jnp.int32, shape, 1)


def gram_kernel(
    place_ref, own_ref, side_ref, below_ref, cross_ref, out_ref, diagonal_ref, block_ref
):
    row = place_ref[0]
    col = place_ref[1]
    place_quads(row, col, (own_ref, side_ref, below_ref, cross_ref), block_ref)

    def emit(left_gram, which):
        def product(first, second):
            a = slice(first * GB, (first + 1) * GB)
            b = slice(second * GB, (second + 1) * GB)
            if left_gram:
                return dot_nt(block_ref[a, :], block_ref[b, :])
            return dot_tn(block_ref[:, a], block_ref[:, b])

        r, c = grid_positions()
        upper = product(2 * which, 2 * which)
        lower = product(2 * which + 1, 2 * which + 1)
        diagonal = jnp.sum(jnp.where(r == c, lower, 0.0), axis=0, keepdims=True)
        tile_row = lax.broadcasted_iota(jnp.int32, (SUB, 128), 0)
        diagonal_ref[...] = jnp.where(
            tile_row == 0, diagonal[:, :128], jnp.where(tile_row == 1, diagonal[:, 128:], 0.0)
        ).astype(jnp.bfloat16)
        for n in range(4):
            if n < 3:
                value = product(*ABOVE[which][n])
            else:
                value = jnp.where(r <= c, upper, lower)
            for half in range(2):
                tiles = value[:, half * 128 : (half + 1) * 128].reshape(GB // SUB, SUB, 128)
                span = slice(n % 2 * 128, (n % 2 + 1) * 128)
                out_ref[:, 2 * half + n // 2, :, span] = tiles.astype(jnp.bfloat16)

    for left_gram in (True, False):
        for which in range(2):
            pl.when((col == (0 if left_gram else 1)) & (row == which))(
                functools.partial(emit, left_gram, which)
            )


def gram_pieces(place, quads):
    size = 2 * quads[0].shape[0]
    return pl.pallas_call(
        gram_kernel,
        in_specs=[whole(pltpu.SMEM)] + [whole()] * 4,
        out_specs=[whole()] * 2,
        out_shape=[
            jax.ShapeDtypeStruct((32, 4, SUB, WIDTH), jnp.bfloat16),
            jax.ShapeDtypeStruct((SUB, 128), jnp.bfloat16),
        ],
        scratch_shapes=[pltpu.VMEM((size, size), jnp.bfloat16)],
        compiler_params=PARAMS,
        cost_estimate=pl.CostEstimate(
            flops=36 * 10**9, bytes_accessed=3 * 10**6, transcendentals=0
        ),
        name="gram_pieces",
    )(place, *quads)


GROUPS = 4


def second_kernel(codes_ref, rows_ref, gram_ref, out_ref, live_ref, arranged_ref, sems):
    items = live_ref.shape[0] // GROUPS
    dests = arranged_ref.shape[0] // GROUPS
    pieces = pltpu.make_async_copy(gram_ref, arranged_ref.at[:, :, 768:1024], sems.at[2 * GROUPS])
    for group in range(GROUPS):

        @pl.loop(items * group, items * (group + 1))
        def _(item, group=group):
            pltpu.make_async_copy(
                rows_ref.at[codes_ref[item]], live_ref.at[item], sems.at[group]
            ).start()

    pieces.start()
    stores = []
    for group in range(GROUPS):
        pltpu.make_async_copy(
            rows_ref.at[0:items], live_ref.at[items * group : items * (group + 1)], sems.at[group]
        ).wait()

        @pl.loop(items // 2 * group, items // 2 * (group + 1))
        def _(block):
            left = live_ref[2 * block]
            right = live_ref[2 * block + 1]
            base = (block // 4) * 16 + (block % 4) * 2
            for i in range(2):
                at = base + 8 * i
                arranged_ref[at, :, 0:512] = left[:, 512 * i : 512 * (i + 1)]
                arranged_ref[at, :, 512:768] = right[:, 0:256]
                arranged_ref[at + 1, :, 0:768] = right[:, 256:1024]

        if group == 0:
            pieces.wait()
        span = slice(dests * group, dests * (group + 1))
        store = pltpu.make_async_copy(
            arranged_ref.at[span], out_ref.at[span], sems.at[GROUPS + group]
        )
        store.start()
        stores.append(store)
    for store in stores:
        store.wait()


def second_operand(codes, rows, gram):
    return pl.pallas_call(
        second_kernel,
        in_specs=[whole(pltpu.SMEM), whole(pl.ANY), whole(pl.ANY)],
        out_specs=whole(pl.ANY),
        out_shape=jax.ShapeDtypeStruct((128, SUB, 1024), jnp.bfloat16),
        scratch_shapes=[
            pltpu.VMEM((64, SUB, 1024), jnp.bfloat16),
            pltpu.VMEM((128, SUB, 1024), jnp.bfloat16),
            pltpu.SemaphoreType.DMA((2 * GROUPS + 1,)),
        ],
        compiler_params=pltpu.CompilerParams(vmem_limit_bytes=8 * 2**20),
        cost_estimate=pl.CostEstimate(flops=0, bytes_accessed=8 * 10**6, transcendentals=0),
        name="second_operand",
    )(codes, rows, gram)


def third_kernel(
    codes_ref, mine_ref, got_ref, diagonal_ref, out_ref, held_ref, packed_ref, sems
):
    items = packed_ref.shape[0] // GROUPS
    sources = held_ref.shape[0] // GROUPS
    loads = []
    for group in range(GROUPS):
        span = slice(sources * group, sources * (group + 1))
        load = pltpu.make_async_copy(
            got_ref.at[span, :, 768:1024], held_ref.at[span], sems.at[group]
        )
        load.start()
        loads.append(load)
    apart = pltpu.make_async_copy(
        diagonal_ref,
        out_ref.at[codes_ref[mine_ref[0]] // 2, :, 4 * WIDTH : 4 * WIDTH + 128],
        sems.at[2 * GROUPS],
    )
    apart.start()
    for group in range(GROUPS):
        loads[group].wait()

        @pl.loop(items * group, items * (group + 1))
        def _(item, group=group):
            block = item // 2
            upper = (block // 4) * 16 + (block % 4) * 2 + item % 2
            packed_ref[item, :, 0:WIDTH] = held_ref[upper]
            packed_ref[item, :, WIDTH:] = held_ref[upper + 8]
            code = codes_ref[item]
            lane = pl.multiple_of(code % 2 * (2 * WIDTH), 2 * WIDTH)
            pltpu.make_async_copy(
                packed_ref.at[item],
                out_ref.at[code // 2, :, pl.ds(lane, 2 * WIDTH)],
                sems.at[GROUPS + group],
            ).start()

    for group in range(GROUPS):
        span = slice(items * group, items * (group + 1))
        pltpu.make_async_copy(
            packed_ref.at[span], out_ref.at[span, :, 0 : 2 * WIDTH], sems.at[GROUPS + group]
        ).wait()
    apart.wait()


def third_operand(codes, my_item, got, diagonal):
    return pl.pallas_call(
        third_kernel,
        in_specs=[whole(pltpu.SMEM), whole(pltpu.SMEM), whole(pl.ANY), whole(pl.ANY)],
        out_specs=whole(pl.ANY),
        out_shape=pltpu.HBM((128, SUB, 4 * WIDTH + 128), jnp.bfloat16),
        scratch_shapes=[
            pltpu.VMEM((128, SUB, WIDTH), jnp.bfloat16),
            pltpu.VMEM((64, SUB, 2 * WIDTH), jnp.bfloat16),
            pltpu.SemaphoreType.DMA((2 * GROUPS + 1,)),
        ],
        compiler_params=pltpu.CompilerParams(vmem_limit_bytes=8 * 2**20),
        cost_estimate=pl.CostEstimate(flops=0, bytes_accessed=4 * 10**6, transcendentals=0),
        name="third_operand",
    )(codes, my_item, got, diagonal)


def rotate_kernel(
    place_ref,
    own_ref,
    side_ref,
    below_ref,
    cross_ref,
    mine_ref,
    theirs_ref,
    first_ref,
    second_ref,
    new_first_ref,
    new_second_ref,
    direction_ref,
    block_ref,
    left_ref,
    right_ref,
):
    row = place_ref[0]
    col = place_ref[1]
    place_quads(row, col, (own_ref, side_ref, below_ref, cross_ref), block_ref)

    @pl.when(col == 0)
    def _():
        left_ref[...] = mine_ref[:, :, 0:512]
        right_ref[:, :, 0:256] = mine_ref[:, :, 512:768]
        right_ref[:, :, 256:512] = theirs_ref[:, :, 0:256]

    @pl.when(col == 1)
    def _():
        left_ref[...] = theirs_ref[:, :, 0:512]
        right_ref[...] = mine_ref[:, :, 256:768]

    left = left_ref[...].reshape(1024, 512)
    left_rot = dot_tn(left, block_ref[...]).astype(jnp.bfloat16)
    rotated = dot_nn(left_rot, right_ref[...].reshape(1024, 512))
    new_first = beta_one * first_ref[...] + (1.0 - beta_one) * rotated
    new_second = beta_two * second_ref[...] + (1.0 - beta_two) * rotated * rotated
    new_first_ref[...] = new_first
    new_second_ref[...] = new_second
    direction_ref[...] = (new_first / (jnp.sqrt(new_second) + epsilon)).astype(jnp.bfloat16)


def rotate(place, quads, mine, theirs, first, second):
    half = first.shape[0]
    return pl.pallas_call(
        rotate_kernel,
        grid=(1,),
        in_specs=[whole(pltpu.SMEM)]
        + [pl.BlockSpec((half, half), lambda _: (0, 0))] * 4
        + [pl.BlockSpec((128, SUB, 768), lambda _: (0, 0, 0))] * 2
        + [pl.BlockSpec((half, half), lambda _: (0, 0))] * 2,
        out_specs=[pl.BlockSpec((half, half), lambda _: (0, 0))] * 3,
        out_shape=[
            jax.ShapeDtypeStruct((half, half), jnp.float32),
            jax.ShapeDtypeStruct((half, half), jnp.float32),
            jax.ShapeDtypeStruct((half, half), jnp.bfloat16),
        ],
        scratch_shapes=[
            pltpu.VMEM((1024, 1024), jnp.bfloat16),
            pltpu.VMEM((128, SUB, 512), jnp.bfloat16),
            pltpu.VMEM((128, SUB, 512), jnp.bfloat16),
        ],
        compiler_params=PARAMS,
        cost_estimate=pl.CostEstimate(
            flops=16 * 10**8, bytes_accessed=10**7, transcendentals=10**6
        ),
        name="rotate",
    )(place, *quads, mine, theirs, first, second)


def back_kernel(
    place_ref,
    own_ref,
    side_ref,
    mine_ref,
    theirs_ref,
    keep_ref,
    give_ref,
    left_ref,
    right_ref,
    strip_ref,
):
    row = place_ref[0]
    col = place_ref[1]
    half = own_ref.shape[0]
    strip_ref[:, pl.ds(pl.multiple_of(col * half, half), half)] = own_ref[...]
    strip_ref[:, pl.ds(pl.multiple_of((1 - col) * half, half), half)] = side_ref[...]

    @pl.when(col == 0)
    def _():
        left_ref[...] = mine_ref[:, :, 0:512]
        right_ref[:, :, 0:256] = mine_ref[0:64, :, 512:768]
        right_ref[:, :, 256:1024] = theirs_ref[0:64]

    @pl.when(col == 1)
    def _():
        left_ref[...] = theirs_ref[:, :, 0:512]
        right_ref[:, :, 0:256] = theirs_ref[64:128, :, 512:768]
        right_ref[:, :, 256:1024] = mine_ref[64:128]

    half_back = dot_nt(strip_ref[...], right_ref[...].reshape(512, 1024)).astype(jnp.bfloat16)
    groups = half // SUB
    keep = left_ref[pl.ds(row * groups, groups)].reshape(half, 512)
    give = left_ref[pl.ds((1 - row) * groups, groups)].reshape(half, 512)
    keep_ref[...] = dot_nn(keep, half_back)
    give_ref[...] = dot_nn(give, half_back).astype(jnp.bfloat16)


def back(place, own, side, mine, theirs):
    half = own.shape[0]
    return pl.pallas_call(
        back_kernel,
        grid=(1,),
        in_specs=[whole(pltpu.SMEM)]
        + [pl.BlockSpec((half, half), lambda _: (0, 0))] * 2
        + [pl.BlockSpec((128, SUB, 768), lambda _: (0, 0, 0))] * 2,
        out_specs=[pl.BlockSpec((half, half), lambda _: (0, 0))] * 2,
        out_shape=[
            jax.ShapeDtypeStruct((half, half), jnp.float32),
            jax.ShapeDtypeStruct((half, half), jnp.bfloat16),
        ],
        scratch_shapes=[
            pltpu.VMEM((128, SUB, 512), jnp.bfloat16),
            pltpu.VMEM((64, SUB, 1024), jnp.bfloat16),
            pltpu.VMEM((half, 2 * half), jnp.bfloat16),
        ],
        compiler_params=PARAMS,
        cost_estimate=pl.CostEstimate(flops=11 * 10**8, bytes_accessed=6 * 10**6, transcendentals=0),
        name="back",
    )(place, own, side, mine, theirs)


def factor_kernel(
    items_ref, live_ref, factor_ref, got_ref, out_ref, strips_ref, held_ref, sems
):
    slots = factor_ref.shape[0]
    count = 4 * slots

    def at(n):
        return (n // 4, slice(GB * (n % 4), GB * (n % 4 + 1)))

    pieces = pltpu.make_async_copy(got_ref, held_ref, sems.at[2 * count])
    loads = [
        pltpu.make_async_copy(factor_ref.at[at(n)], strips_ref.at[n], sems.at[n])
        for n in range(count)
    ]
    stores = [
        pltpu.make_async_copy(strips_ref.at[n], out_ref.at[at(n)], sems.at[count + n])
        for n in range(count)
    ]
    loads[0].start()
    pieces.start()
    for n in range(1, count):
        loads[n].start()

    def piece(slot, which, n):
        lane = 2 * WIDTH * slot + (2 * which + n % 2) * 128
        halves = [
            held_ref[:, 2 * h + n // 2, :, lane : lane + 128]
            .astype(jnp.float32)
            .reshape(GB, 128)
            for h in range(2)
        ]
        return jnp.concatenate(halves, axis=1)

    def sub_block(slot, row, col):
        if row != col:
            pair = (min(row, col), max(row, col))
            which = 0 if pair in ABOVE[0] else 1
            value = piece(slot, which, ABOVE[which].index(pair))
            return value if row < col else value.T
        value = piece(slot, row // 2, 3)
        r, c = grid_positions()
        if row % 2 == 0:
            return jnp.where(r <= c, value, value.T)
        item = items_ref[slot]
        block = item // 2
        source = (block // 4 * 2 + row // 2) * 8 + block % 4 * 2 + item % 2
        tile = held_ref[source // 4, source % 4, :, 4 * WIDTH :].astype(jnp.float32)
        diagonal = jnp.concatenate([tile[0:1], tile[1:2]], axis=1)
        return jnp.where(r > c, value, jnp.where(r < c, value.T, diagonal))

    def mix(n):
        slot, row = n // 4, n % 4
        for col in range(4):
            span = slice(col * GB, (col + 1) * GB)
            strips_ref[n, :, span] = shampoo_beta * strips_ref[n, :, span] + (
                1.0 - shampoo_beta
            ) * sub_block(slot, row, col)

    for n in range(count):
        loads[n].wait()
        if n == 0:
            pieces.wait()
        pl.when(live_ref[n // 4] != 0)(functools.partial(mix, n))
        stores[n].start()
    for n in range(count):
        stores[n].wait()


def update_factors(items, live, factors, got):
    slots, size, _ = factors.shape
    got = got.reshape(32, 4, SUB, got.shape[2])
    return pl.pallas_call(
        factor_kernel,
        in_specs=[whole(pltpu.SMEM)] * 2 + [whole(pl.ANY)] * 2,
        out_specs=whole(pl.ANY),
        out_shape=jax.ShapeDtypeStruct(factors.shape, factors.dtype),
        scratch_shapes=[
            pltpu.VMEM((4 * slots, GB, size), jnp.float32),
            pltpu.VMEM(got.shape, got.dtype),
            pltpu.SemaphoreType.DMA((8 * slots + 1,)),
        ],
        compiler_params=pltpu.CompilerParams(vmem_limit_bytes=20 * 2**20),
        cost_estimate=pl.CostEstimate(
            flops=4 * 10**6, bytes_accessed=2 * 10**7, transcendentals=0
        ),
        name="update_factors",
    )(items, live, pltpu.with_memory_space_constraint(factors, pltpu.HBM), got)


def shards(gradient, first_moment, second_moment, factors, eigen_bases, owners):
    devices = lax.axis_size("fsdp") * lax.axis_size("rep")
    slots = factors.shape[0]
    size = factors.shape[1]
    item_count = owners.shape[0]
    fsdp_index = lax.axis_index("fsdp")
    rep_index = lax.axis_index("rep")
    my_index = fsdp_index * lax.axis_size("rep") + rep_index
    my_item = (fsdp_index // 2 * 8 + rep_index).reshape(1).astype(jnp.int32)
    place = jnp.stack([fsdp_index % 2, rep_index % 2]).astype(jnp.int32)

    below = swap_neighbour(gradient, "fsdp")
    first_parts = interleave(eigen_bases, devices)
    first_got = lax.all_to_all(first_parts, BOTH, 0, 0, tiled=True)

    item_index = jnp.arange(item_count, dtype=jnp.int32)
    earlier_same = (owners[:, None] == owners[None, :]) & (
        item_index[None, :] < item_index[:, None]
    )
    codes = slots * owners + jnp.sum(earlier_same.astype(jnp.int32), axis=1)
    my_codes = my_index * slots + jnp.arange(slots, dtype=jnp.int32)
    hits = (codes[None, :] == my_codes[:, None]).astype(jnp.int32)
    live = jnp.sum(hits, axis=1)
    items = jnp.sum(hits * item_index[None, :], axis=1)

    side = swap_neighbour(gradient, "rep")
    cross = swap_neighbour(below, "rep")
    quads = (gradient, side, below, cross)
    gram, diagonal = gram_pieces(place, quads)
    gram = gram.reshape(devices, SUB, WIDTH)

    second_parts = second_operand(codes, first_got.reshape(devices * slots, SUB, size), gram)
    mine = lax.all_to_all(second_parts, BOTH, 0, 0, tiled=True)
    theirs = swap_neighbour(mine, "rep")

    third_parts = third_operand(codes, my_item, mine, diagonal)
    third_got = lax.all_to_all(third_parts, BOTH, 0, 0, tiled=True)

    new_first, new_second, direction = rotate(
        place, quads, mine, theirs, first_moment, second_moment
    )
    other = swap_neighbour(direction, "rep")
    keep, give = back(place, direction, other, mine, theirs)
    update = keep + swap_neighbour(give, "fsdp").astype(jnp.float32)
    new_factors = update_factors(items, live, factors, third_got)
    return (update, new_first, new_second, new_factors)


def solution(mesh):
    in_specs = (
        P("fsdp", "rep"),
        P("fsdp", "rep"),
        P("fsdp", "rep"),
        P(("fsdp", "rep"), None, None),
        P(("fsdp", "rep"), None, None),
        P(),
    )
    out_specs = (
        P("fsdp", "rep"),
        P("fsdp", "rep"),
        P("fsdp", "rep"),
        P(("fsdp", "rep"), None, None),
    )
    return jax.shard_map(shards, mesh=mesh, in_specs=in_specs, out_specs=out_specs, check_vma=False)
```

```python
import functools

import jax
import jax.numpy as jnp
from jax import lax
from jax.experimental import pallas as pl
from jax.experimental.pallas import tpu as pltpu
from jax.sharding import PartitionSpec as P

beta_one = 0.9
beta_two = 0.95
shampoo_beta = 0.95
epsilon = 1e-08

SUB = 8
GB = 256
ABOVE = (((0, 1), (0, 2), (0, 3)), ((1, 2), (1, 3), (2, 3)))
WIDTH = 2 * 128
BOTH = ("fsdp", "rep")
PARAMS = pltpu.CompilerParams(vmem_limit_bytes=24 * 2**20)


def swap_neighbour(value, axis):
    pairs = [(source, source ^ 1) for source in range(lax.axis_size(axis))]
    return lax.ppermute(value, axis, pairs)


def dot_nn(left, right):
    return jnp.dot(left, right, preferred_element_type=jnp.float32)


def dot_tn(left, right):
    return lax.dot_general(
        left, right, (((0,), (0,)), ((), ())), preferred_element_type=jnp.float32
    )


def dot_nt(left, right):
    return lax.dot_general(
        left, right, (((1,), (1,)), ((), ())), preferred_element_type=jnp.float32
    )


def whole(memory_space=pltpu.VMEM):
    return pl.BlockSpec(memory_space=memory_space)


def interleave_kernel(src_ref, dst_ref, held_ref, sems):
    slots, devices = held_ref.shape[0], held_ref.shape[1]
    stores = []
    loads = []
    for n in range(2 * slots):
        slot, span = n % slots, pl.ds(n // slots * (devices // 2), devices // 2)
        held = held_ref.at[slot, span]
        loads.append(pltpu.make_async_copy(src_ref.at[slot, span], held, sems.at[0, n]))
        stores.append(pltpu.make_async_copy(held, dst_ref.at[span, slot], sems.at[1, n]))
        loads[n].start()
    for load, store in zip(loads, stores):
        load.wait()
        store.start()
    for store in stores:
        store.wait()


def interleave(bases, devices):
    slots, size, _ = bases.shape
    parts = bases.reshape(slots, devices, SUB, size)
    return pl.pallas_call(
        interleave_kernel,
        in_specs=[whole(pl.ANY)],
        out_specs=whole(pl.ANY),
        out_shape=pltpu.HBM((devices, slots, SUB, size), bases.dtype),
        scratch_shapes=[
            pltpu.VMEM(parts.shape, bases.dtype),
            pltpu.SemaphoreType.DMA((2, 2 * slots)),
        ],
        compiler_params=pltpu.CompilerParams(vmem_limit_bytes=8 * 2**20),
        cost_estimate=pl.CostEstimate(flops=0, bytes_accessed=8 * 10**6, transcendentals=0),
        name="interleave",
    )(pltpu.with_memory_space_constraint(parts, pltpu.HBM))


def place_quads(row, col, quads, block_ref):
    half = quads[0].shape[0]
    for dr in range(2):
        for dc in range(2):
            at = (pl.multiple_of((row ^ dr) * half, half), pl.multiple_of((col ^ dc) * half, half))
            block_ref[pl.ds(at[0], half), pl.ds(at[1], half)] = quads[2 * dr + dc][...]


def grid_positions():
    shape = (GB, GB)
    return lax.broadcasted_iota(jnp.int32, shape, 0), lax.broadcasted_iota(jnp.int32, shape, 1)


def gram_kernel(
    place_ref, own_ref, side_ref, below_ref, cross_ref, out_ref, diagonal_ref, block_ref
):
    row = place_ref[0]
    col = place_ref[1]
    place_quads(row, col, (own_ref, side_ref, below_ref, cross_ref), block_ref)

    def emit(left_gram, which):
        def product(first, second):
            a = slice(first * GB, (first + 1) * GB)
            b = slice(second * GB, (second + 1) * GB)
            if left_gram:
                return dot_nt(block_ref[a, :], block_ref[b, :])
            return dot_tn(block_ref[:, a], block_ref[:, b])

        r, c = grid_positions()
        upper = product(2 * which, 2 * which)
        lower = product(2 * which + 1, 2 * which + 1)
        diagonal = jnp.sum(jnp.where(r == c, lower, 0.0), axis=0, keepdims=True)
        tile_row = lax.broadcasted_iota(jnp.int32, (SUB, 128), 0)
        diagonal_ref[...] = jnp.where(
            tile_row == 0, diagonal[:, :128], jnp.where(tile_row == 1, diagonal[:, 128:], 0.0)
        ).astype(jnp.bfloat16)
        for n in range(4):
            if n < 3:
                value = product(*ABOVE[which][n])
            else:
                value = jnp.where(r <= c, upper, lower)
            for half in range(2):
                tiles = value[:, half * 128 : (half + 1) * 128].reshape(GB // SUB, SUB, 128)
                span = slice(n % 2 * 128, (n % 2 + 1) * 128)
                out_ref[:, 2 * half + n // 2, :, span] = tiles.astype(jnp.bfloat16)

    for left_gram in (True, False):
        for which in range(2):
            pl.when((col == (0 if left_gram else 1)) & (row == which))(
                functools.partial(emit, left_gram, which)
            )


def gram_pieces(place, quads):
    size = 2 * quads[0].shape[0]
    return pl.pallas_call(
        gram_kernel,
        in_specs=[whole(pltpu.SMEM)] + [whole()] * 4,
        out_specs=[whole()] * 3,
        out_shape=[
            jax.ShapeDtypeStruct((32, 4, SUB, WIDTH), jnp.bfloat16),
            jax.ShapeDtypeStruct((SUB, 128), jnp.bfloat16),
            pltpu.HBM((size, size), jnp.bfloat16),
        ],
        compiler_params=PARAMS,
        cost_estimate=pl.CostEstimate(
            flops=36 * 10**9, bytes_accessed=3 * 10**6, transcendentals=0
        ),
        name="gram_pieces",
    )(place, *quads)


GROUPS = 4


def second_kernel(codes_ref, rows_ref, gram_ref, out_ref, live_ref, sems):
    items = live_ref.shape[0] // GROUPS
    pieces = pltpu.make_async_copy(gram_ref, out_ref.at[:, :, 768:1024], sems.at[GROUPS])
    for group in range(GROUPS):

        @pl.loop(items * group, items * (group + 1))
        def _(item, group=group):
            pltpu.make_async_copy(
                rows_ref.at[codes_ref[item]], live_ref.at[item], sems.at[group]
            ).start()

    pieces.start()
    for group in range(GROUPS):
        pltpu.make_async_copy(
            rows_ref.at[0:items], live_ref.at[items * group : items * (group + 1)], sems.at[group]
        ).wait()

        @pl.loop(items // 2 * group, items // 2 * (group + 1))
        def _(block):
            left = live_ref[2 * block]
            right = live_ref[2 * block + 1]
            base = (block // 4) * 16 + (block % 4) * 2
            for i in range(2):
                at = base + 8 * i
                out_ref[at, :, 0:512] = left[:, 512 * i : 512 * (i + 1)]
                out_ref[at, :, 512:768] = right[:, 0:256]
                out_ref[at + 1, :, 0:768] = right[:, 256:1024]

    pieces.wait()


def second_operand(codes, rows, gram):
    return pl.pallas_call(
        second_kernel,
        in_specs=[whole(pltpu.SMEM), whole(pl.ANY), whole(pl.ANY)],
        out_specs=whole(),
        out_shape=pltpu.VMEM((128, SUB, 1024), jnp.bfloat16),
        scratch_shapes=[
            pltpu.VMEM((64, SUB, 1024), jnp.bfloat16),
            pltpu.SemaphoreType.DMA((GROUPS + 1,)),
        ],
        compiler_params=pltpu.CompilerParams(vmem_limit_bytes=8 * 2**20),
        cost_estimate=pl.CostEstimate(flops=0, bytes_accessed=8 * 10**6, transcendentals=0),
        name="second_operand",
    )(codes, rows, gram)


def third_kernel(codes_ref, mine_ref, got_ref, diagonal_ref, out_ref, sems):
    apart = pltpu.make_async_copy(
        diagonal_ref,
        out_ref.at[codes_ref[mine_ref[0]] // 2, :, 4 * WIDTH : 4 * WIDTH + 128],
        sems.at[0],
    )
    apart.start()

    @pl.loop(0, 32)
    def _(block):
        for side in range(2):
            code = codes_ref[2 * block + side]
            for half in range(2):
                source = (block // 4) * 16 + (block % 4) * 2 + side + 8 * half
                lane = pl.multiple_of(code % 2 * (2 * WIDTH) + half * WIDTH, WIDTH)
                pltpu.make_async_copy(
                    got_ref.at[source, :, 768:1024],
                    out_ref.at[code // 2, :, pl.ds(lane, WIDTH)],
                    sems.at[1],
                ).start()

    pltpu.make_async_copy(
        got_ref.at[:, :, 768:1024], out_ref.at[:, :, 0:WIDTH], sems.at[1]
    ).wait()
    apart.wait()


def third_operand(codes, my_item, got, diagonal):
    return pl.pallas_call(
        third_kernel,
        in_specs=[whole(pltpu.SMEM), whole(pltpu.SMEM), whole(pl.ANY), whole(pl.ANY)],
        out_specs=whole(pl.ANY),
        out_shape=pltpu.HBM((128, SUB, 4 * WIDTH + 128), jnp.bfloat16),
        scratch_shapes=[pltpu.SemaphoreType.DMA((2,))],
        compiler_params=pltpu.CompilerParams(vmem_limit_bytes=8 * 2**20),
        cost_estimate=pl.CostEstimate(flops=0, bytes_accessed=4 * 10**6, transcendentals=0),
        name="third_operand",
    )(codes, my_item, pltpu.with_memory_space_constraint(got, pltpu.VMEM), diagonal)


def rotate_kernel(
    place_ref,
    block_ref,
    mine_ref,
    theirs_ref,
    first_ref,
    second_ref,
    new_first_ref,
    new_second_ref,
    direction_ref,
    held_ref,
    left_ref,
    right_ref,
    moment_ref,
    sems,
):
    col = place_ref[1]
    to_left = left_ref
    to_right = [right_ref.at[:, :, 256 * n : 256 * (n + 1)] for n in range(2)]

    def load(source, target, n):
        return pltpu.make_async_copy(source, target, sems.at[n])

    @pl.when(col == 0)
    def _():
        load(mine_ref.at[:, :, 0:512], to_left, 0).start()
        load(mine_ref.at[:, :, 512:768], to_right[0], 1).start()
        load(theirs_ref.at[:, :, 0:256], to_right[1], 2).start()

    @pl.when(col == 1)
    def _():
        load(theirs_ref.at[:, :, 0:512], to_left, 0).start()
        load(mine_ref.at[:, :, 256:512], to_right[0], 1).start()
        load(mine_ref.at[:, :, 512:768], to_right[1], 2).start()

    load_block = load(block_ref, held_ref, 3)
    load_block.start()
    moments = [load(first_ref, moment_ref.at[0], 4), load(second_ref, moment_ref.at[1], 5)]
    for moment in moments:
        moment.start()
    load(mine_ref.at[:, :, 0:512], to_left, 0).wait()
    load_block.wait()
    size = held_ref.shape[0]
    left_rot = dot_tn(left_ref[...].reshape(size, 512), held_ref[...]).astype(jnp.bfloat16)
    for n in range(2):
        load(mine_ref.at[:, :, 0:256], to_right[n], 1 + n).wait()
    for moment in moments:
        moment.wait()
    right = right_ref[...].reshape(size, 512)
    stores = []
    for part in range(4):
        rows = slice(128 * part, 128 * (part + 1))
        rotated = dot_nn(left_rot[rows], right)
        new_first = beta_one * moment_ref[0, rows] + (1.0 - beta_one) * rotated
        new_second = beta_two * moment_ref[1, rows] + (1.0 - beta_two) * rotated * rotated
        direction_ref[rows] = (new_first / (jnp.sqrt(new_second) + epsilon)).astype(jnp.bfloat16)
        moment_ref[0, rows] = new_first
        moment_ref[1, rows] = new_second
        for n, target in enumerate((new_first_ref, new_second_ref)):
            store = load(moment_ref.at[n, rows], target.at[rows], 6 + 2 * part + n)
            store.start()
            stores.append(store)
    for store in stores:
        store.wait()


def rotate(place, block, mine, theirs, first, second):
    half = first.shape[0]
    block, first, second = (
        pltpu.with_memory_space_constraint(value, pltpu.HBM) for value in (block, first, second)
    )
    return pl.pallas_call(
        rotate_kernel,
        in_specs=[whole(pltpu.SMEM)] + [whole(pl.ANY)] * 5,
        out_specs=[whole(pl.ANY), whole(pl.ANY), whole()],
        out_shape=[
            jax.ShapeDtypeStruct((half, half), jnp.float32),
            jax.ShapeDtypeStruct((half, half), jnp.float32),
            jax.ShapeDtypeStruct((half, half), jnp.bfloat16),
        ],
        scratch_shapes=[
            pltpu.VMEM((1024, 1024), jnp.bfloat16),
            pltpu.VMEM((128, SUB, 512), jnp.bfloat16),
            pltpu.VMEM((128, SUB, 512), jnp.bfloat16),
            pltpu.VMEM((2, half, half), jnp.float32),
            pltpu.SemaphoreType.DMA((14,)),
        ],
        compiler_params=pltpu.CompilerParams(vmem_limit_bytes=20 * 2**20),
        cost_estimate=pl.CostEstimate(
            flops=16 * 10**8, bytes_accessed=10**7, transcendentals=10**6
        ),
        name="rotate",
    )(place, block, mine, theirs, first, second)


def back_kernel(
    place_ref,
    own_ref,
    side_ref,
    mine_ref,
    theirs_ref,
    keep_ref,
    give_ref,
    left_ref,
    right_ref,
    strip_ref,
):
    row = place_ref[0]
    col = place_ref[1]
    half = own_ref.shape[0]
    strip_ref[:, pl.ds(pl.multiple_of(col * half, half), half)] = own_ref[...]
    strip_ref[:, pl.ds(pl.multiple_of((1 - col) * half, half), half)] = side_ref[...]

    @pl.when(col == 0)
    def _():
        left_ref[...] = mine_ref[:, :, 0:512]
        right_ref[:, :, 0:256] = mine_ref[0:64, :, 512:768]
        right_ref[:, :, 256:1024] = theirs_ref[0:64]

    @pl.when(col == 1)
    def _():
        left_ref[...] = theirs_ref[:, :, 0:512]
        right_ref[:, :, 0:256] = theirs_ref[64:128, :, 512:768]
        right_ref[:, :, 256:1024] = mine_ref[64:128]

    half_back = dot_nt(strip_ref[...], right_ref[...].reshape(512, 1024)).astype(jnp.bfloat16)
    groups = half // SUB
    keep = left_ref[pl.ds(row * groups, groups)].reshape(half, 512)
    give = left_ref[pl.ds((1 - row) * groups, groups)].reshape(half, 512)
    keep_ref[...] = dot_nn(keep, half_back)
    give_ref[...] = dot_nn(give, half_back).astype(jnp.bfloat16)


def back(place, own, side, mine, theirs):
    half = own.shape[0]
    return pl.pallas_call(
        back_kernel,
        grid=(1,),
        in_specs=[whole(pltpu.SMEM)]
        + [pl.BlockSpec((half, half), lambda _: (0, 0))] * 2
        + [pl.BlockSpec((128, SUB, 768), lambda _: (0, 0, 0))] * 2,
        out_specs=[pl.BlockSpec((half, half), lambda _: (0, 0))] * 2,
        out_shape=[
            jax.ShapeDtypeStruct((half, half), jnp.float32),
            jax.ShapeDtypeStruct((half, half), jnp.bfloat16),
        ],
        scratch_shapes=[
            pltpu.VMEM((128, SUB, 512), jnp.bfloat16),
            pltpu.VMEM((64, SUB, 1024), jnp.bfloat16),
            pltpu.VMEM((half, 2 * half), jnp.bfloat16),
        ],
        compiler_params=PARAMS,
        cost_estimate=pl.CostEstimate(flops=11 * 10**8, bytes_accessed=6 * 10**6, transcendentals=0),
        name="back",
    )(place, own, side, mine, theirs)


def settle_kernel(factor_ref, out_ref, strips_ref, sems):
    count = strips_ref.shape[0]
    loads = [
        pltpu.make_async_copy(factor_ref.at[strip_of(n)], strips_ref.at[n], sems.at[0, n])
        for n in range(count)
    ]
    stores = [
        pltpu.make_async_copy(strips_ref.at[n], out_ref.at[strip_of(n)], sems.at[1, n])
        for n in range(count)
    ]
    for load in loads:
        load.start()
    for load, store in zip(loads, stores):
        load.wait()
        store.start()
    for store in stores:
        store.wait()


def settle(factors):
    slots, size, _ = factors.shape
    return pl.pallas_call(
        settle_kernel,
        in_specs=[whole(pl.ANY)],
        out_specs=whole(pl.ANY),
        out_shape=pltpu.HBM(factors.shape, factors.dtype),
        scratch_shapes=[
            pltpu.VMEM((4 * slots, GB, size), jnp.float32),
            pltpu.SemaphoreType.DMA((2, 4 * slots)),
        ],
        compiler_params=pltpu.CompilerParams(vmem_limit_bytes=12 * 2**20),
        cost_estimate=pl.CostEstimate(
            flops=0, bytes_accessed=16 * 10**6, transcendentals=0
        ),
        name="settle",
    )(pltpu.with_memory_space_constraint(factors, pltpu.HBM))


def strip_of(n):
    return (n // 4, slice(GB * (n % 4), GB * (n % 4 + 1)))


def factor_kernel(
    items_ref, live_ref, factor_ref, got_ref, out_ref, strips_ref, held_ref, sems
):
    slots = factor_ref.shape[0]
    count = 4 * slots
    spans = [slice(2 * WIDTH * slot, 2 * WIDTH * (slot + 1)) for slot in range(slots)]
    spans.append(slice(2 * WIDTH * slots, got_ref.shape[3]))
    pieces = [
        pltpu.make_async_copy(
            got_ref.at[:, :, :, span], held_ref.at[:, :, :, span], sems.at[2 * count + n]
        )
        for n, span in enumerate(spans)
    ]
    loads = [
        pltpu.make_async_copy(out_ref.at[strip_of(n)], strips_ref.at[n], sems.at[n])
        for n in range(count)
    ]
    stores = [
        pltpu.make_async_copy(strips_ref.at[n], out_ref.at[strip_of(n)], sems.at[count + n])
        for n in range(count)
    ]
    for slot in range(slots):

        @pl.when(live_ref[slot] != 0)
        def _(slot=slot):
            pieces[slot].start()
            if slot == 0:
                pieces[slots].start()
            for n in range(4 * slot, 4 * (slot + 1)):
                loads[n].start()

    def piece(slot, which, n):
        lane = 2 * WIDTH * slot + (2 * which + n % 2) * 128
        halves = [
            held_ref[:, 2 * h + n // 2, :, lane : lane + 128]
            .astype(jnp.float32)
            .reshape(GB, 128)
            for h in range(2)
        ]
        return jnp.concatenate(halves, axis=1)

    def sub_block(slot, row, col):
        if row != col:
            pair = (min(row, col), max(row, col))
            which = 0 if pair in ABOVE[0] else 1
            value = piece(slot, which, ABOVE[which].index(pair))
            return value if row < col else value.T
        value = piece(slot, row // 2, 3)
        r, c = grid_positions()
        if row % 2 == 0:
            return jnp.where(r <= c, value, value.T)
        item = items_ref[slot]
        block = item // 2
        source = (block // 4 * 2 + row // 2) * 8 + block % 4 * 2 + item % 2
        tile = held_ref[source // 4, source % 4, :, 4 * WIDTH :].astype(jnp.float32)
        diagonal = jnp.concatenate([tile[0:1], tile[1:2]], axis=1)
        return jnp.where(r > c, value, jnp.where(r < c, value.T, diagonal))

    def mix(n):
        slot, row = n // 4, n % 4
        for col in range(4):
            span = slice(col * GB, (col + 1) * GB)
            strips_ref[n, :, span] = shampoo_beta * strips_ref[n, :, span] + (
                1.0 - shampoo_beta
            ) * sub_block(slot, row, col)

    for n in range(count):

        @pl.when(live_ref[n // 4] != 0)
        def _(n=n):
            if n % 4 == 0:
                pieces[n // 4].wait()
            if n == 0:
                pieces[slots].wait()
            loads[n].wait()
            mix(n)
            stores[n].start()

    for n in range(count):
        pl.when(live_ref[n // 4] != 0)(stores[n].wait)


def update_factors(items, live, factors, got):
    slots, size, _ = factors.shape
    got = got.reshape(32, 4, SUB, got.shape[2])
    return pl.pallas_call(
        factor_kernel,
        in_specs=[whole(pltpu.SMEM)] * 2 + [whole(pl.ANY)] * 2,
        out_specs=whole(pl.ANY),
        out_shape=pltpu.HBM(factors.shape, factors.dtype),
        scratch_shapes=[
            pltpu.VMEM((4 * slots, GB, size), jnp.float32),
            pltpu.VMEM(got.shape, got.dtype),
            pltpu.SemaphoreType.DMA((9 * slots + 1,)),
        ],
        input_output_aliases={2: 0},
        compiler_params=pltpu.CompilerParams(vmem_limit_bytes=20 * 2**20),
        cost_estimate=pl.CostEstimate(
            flops=4 * 10**6, bytes_accessed=2 * 10**7, transcendentals=0
        ),
        name="update_factors",
    )(items, live, pltpu.with_memory_space_constraint(factors, pltpu.HBM), got)


def shards(gradient, first_moment, second_moment, factors, eigen_bases, owners):
    devices = lax.axis_size("fsdp") * lax.axis_size("rep")
    slots = factors.shape[0]
    size = factors.shape[1]
    item_count = owners.shape[0]
    fsdp_index = lax.axis_index("fsdp")
    rep_index = lax.axis_index("rep")
    my_index = fsdp_index * lax.axis_size("rep") + rep_index
    my_item = (fsdp_index // 2 * 8 + rep_index).reshape(1).astype(jnp.int32)
    place = jnp.stack([fsdp_index % 2, rep_index % 2]).astype(jnp.int32)

    below = swap_neighbour(gradient, "fsdp")
    first_parts = interleave(eigen_bases, devices)
    first_got = lax.all_to_all(first_parts, BOTH, 0, 0, tiled=True)

    item_index = jnp.arange(item_count, dtype=jnp.int32)
    earlier_same = (owners[:, None] == owners[None, :]) & (
        item_index[None, :] < item_index[:, None]
    )
    codes = slots * owners + jnp.sum(earlier_same.astype(jnp.int32), axis=1)
    my_codes = my_index * slots + jnp.arange(slots, dtype=jnp.int32)
    hits = (codes[None, :] == my_codes[:, None]).astype(jnp.int32)
    live = jnp.sum(hits, axis=1)
    items = jnp.sum(hits * item_index[None, :], axis=1)

    side = swap_neighbour(gradient, "rep")
    cross = swap_neighbour(below, "rep")
    quads = (gradient, side, below, cross)
    settled = settle(factors)
    gram, diagonal, block = gram_pieces(place, quads)
    gram = gram.reshape(devices, SUB, WIDTH)

    second_parts = second_operand(codes, first_got.reshape(devices * slots, SUB, size), gram)
    mine = lax.all_to_all(second_parts, BOTH, 0, 0, tiled=True)
    theirs = swap_neighbour(mine, "rep")

    third_parts = third_operand(codes, my_item, mine, diagonal)
    third_got = lax.all_to_all(third_parts, BOTH, 0, 0, tiled=True)

    new_first, new_second, direction = rotate(
        place, block, mine, theirs, first_moment, second_moment
    )
    other = swap_neighbour(direction, "rep")
    keep, give = back(place, direction, other, mine, theirs)
    update = keep + swap_neighbour(give, "fsdp").astype(jnp.float32)
    new_factors = update_factors(items, live, settled, third_got)
    return (update, new_first, new_second, new_factors)


def solution(mesh):
    in_specs = (
        P("fsdp", "rep"),
        P("fsdp", "rep"),
        P("fsdp", "rep"),
        P(("fsdp", "rep"), None, None),
        P(("fsdp", "rep"), None, None),
        P(),
    )
    out_specs = (
        P("fsdp", "rep"),
        P("fsdp", "rep"),
        P("fsdp", "rep"),
        P(("fsdp", "rep"), None, None),
    )
    return jax.shard_map(shards, mesh=mesh, in_specs=in_specs, out_specs=out_specs, check_vma=False)
```

```python
import functools

import jax
import jax.numpy as jnp
from jax import lax
from jax.experimental import pallas as pl
from jax.experimental.pallas import tpu as pltpu
from jax.sharding import PartitionSpec as P

beta_one = 0.9
beta_two = 0.95
shampoo_beta = 0.95
epsilon = 1e-08

SUB = 8
GB = 256
ABOVE = (((0, 1), (0, 2), (0, 3)), ((1, 2), (1, 3), (2, 3)))
WIDTH = 2 * 128
CHIPS = 64
ROW, COL, MINE, LIVE, NAMED = 64, 65, 66, 67, 69
BASES = 512 + 1024
BOTH = ("fsdp", "rep")
PARAMS = pltpu.CompilerParams(vmem_limit_bytes=24 * 2**20)


def swap_neighbour(value, axis):
    pairs = [(source, source ^ 1) for source in range(lax.axis_size(axis))]
    return lax.ppermute(value, axis, pairs)


def dot_nn(left, right):
    return jnp.dot(left, right, preferred_element_type=jnp.float32)


def dot_tn(left, right):
    return lax.dot_general(
        left, right, (((0,), (0,)), ((), ())), preferred_element_type=jnp.float32
    )


def dot_nt(left, right):
    return lax.dot_general(
        left, right, (((1,), (1,)), ((), ())), preferred_element_type=jnp.float32
    )


def whole(memory_space=pltpu.VMEM):
    return pl.BlockSpec(memory_space=memory_space)


def interleave_kernel(src_ref, dst_ref, held_ref, sems):
    slots, devices = held_ref.shape[0], held_ref.shape[1]
    stores = []
    loads = []
    for n in range(2 * slots):
        slot, span = n % slots, pl.ds(n // slots * (devices // 2), devices // 2)
        held = held_ref.at[slot, span]
        loads.append(pltpu.make_async_copy(src_ref.at[slot, span], held, sems.at[0, n]))
        stores.append(pltpu.make_async_copy(held, dst_ref.at[span, slot], sems.at[1, n]))
        loads[n].start()
    for load, store in zip(loads, stores):
        load.wait()
        store.start()
    for store in stores:
        store.wait()


def interleave(bases, devices):
    slots, size, _ = bases.shape
    parts = bases.reshape(slots, devices, SUB, size)
    return pl.pallas_call(
        interleave_kernel,
        in_specs=[whole(pl.ANY)],
        out_specs=whole(pl.ANY),
        out_shape=pltpu.HBM((devices, slots, SUB, size), bases.dtype),
        scratch_shapes=[
            pltpu.VMEM(parts.shape, bases.dtype),
            pltpu.SemaphoreType.DMA((2, 2 * slots)),
        ],
        compiler_params=pltpu.CompilerParams(vmem_limit_bytes=8 * 2**20),
        cost_estimate=pl.CostEstimate(flops=0, bytes_accessed=8 * 10**6, transcendentals=0),
        name="interleave",
    )(pltpu.with_memory_space_constraint(parts, pltpu.HBM))


def place_quads(row, col, quads, block_ref):
    half = quads[0].shape[0]
    for dr in range(2):
        for dc in range(2):
            at = (pl.multiple_of((row ^ dr) * half, half), pl.multiple_of((col ^ dc) * half, half))
            block_ref[pl.ds(at[0], half), pl.ds(at[1], half)] = quads[2 * dr + dc][...]


def grid_positions():
    shape = (GB, GB)
    return lax.broadcasted_iota(jnp.int32, shape, 0), lax.broadcasted_iota(jnp.int32, shape, 1)


def gram_kernel(
    place_ref, own_ref, side_ref, below_ref, cross_ref, keep_ref, give_ref, diagonal_ref, block_ref
):
    row = place_ref[0]
    col = place_ref[1]
    place_quads(row, col, (own_ref, side_ref, below_ref, cross_ref), block_ref)

    def emit(left_gram, which):
        def product(first, second):
            a = slice(first * GB, (first + 1) * GB)
            b = slice(second * GB, (second + 1) * GB)
            if left_gram:
                return dot_nt(block_ref[a, :], block_ref[b, :])
            return dot_tn(block_ref[:, a], block_ref[:, b])

        r, c = grid_positions()
        upper = product(2 * which, 2 * which)
        lower = product(2 * which + 1, 2 * which + 1)
        diagonal = jnp.sum(jnp.where(r == c, lower, 0.0), axis=0, keepdims=True)
        tile_row = lax.broadcasted_iota(jnp.int32, (SUB, 128), 0)
        diagonal_ref[...] = jnp.where(
            tile_row == 0, diagonal[:, :128], jnp.where(tile_row == 1, diagonal[:, 128:], 0.0)
        ).astype(jnp.bfloat16)
        for n in range(4):
            if n < 3:
                value = product(*ABOVE[which][n])
            else:
                value = jnp.where(r <= c, upper, lower)
            for half in range(2):
                tiles = value[:, half * 128 : (half + 1) * 128].reshape(GB // SUB, SUB, 128)
                span = slice(n % 2 * 128, (n % 2 + 1) * 128)
                kept = n // 2 == (0 if left_gram else 1)
                target = keep_ref if kept else give_ref
                target[:, half, :, span] = tiles.astype(jnp.bfloat16)

    for left_gram in (True, False):
        for which in range(2):
            pl.when((col == (0 if left_gram else 1)) & (row == which))(
                functools.partial(emit, left_gram, which)
            )


def gram_pieces(place, quads):
    size = 2 * quads[0].shape[0]
    return pl.pallas_call(
        gram_kernel,
        in_specs=[whole(pltpu.SMEM)] + [whole()] * 4,
        out_specs=[whole()] * 4,
        out_shape=[
            jax.ShapeDtypeStruct((32, 2, SUB, WIDTH), jnp.bfloat16),
            jax.ShapeDtypeStruct((32, 2, SUB, WIDTH), jnp.bfloat16),
            jax.ShapeDtypeStruct((SUB, 128), jnp.bfloat16),
            pltpu.HBM((size, size), jnp.bfloat16),
        ],
        compiler_params=PARAMS,
        cost_estimate=pl.CostEstimate(
            flops=32 * 10**9, bytes_accessed=3 * 10**6, transcendentals=0
        ),
        name="gram_pieces",
    )(place, *quads)


GROUPS = 4


def second_kernel(facts_ref, rows_ref, keep_ref, other_ref, out_ref, live_ref, sems):
    core = facts_ref[COL]
    items = live_ref.shape[0] // GROUPS
    pieces = []
    for n, source in enumerate((keep_ref, other_ref)):
        lane = pl.multiple_of(BASES + WIDTH * (core ^ n), WIDTH)
        pieces.append(
            pltpu.make_async_copy(
                source, out_ref.at[:, :, pl.ds(lane, WIDTH)], sems.at[GROUPS + n]
            )
        )
    for group in range(GROUPS):

        @pl.loop(items * group, items * (group + 1), unroll=True)
        def _(item, group=group):
            pltpu.make_async_copy(
                rows_ref.at[facts_ref[item]], live_ref.at[item], sems.at[group]
            ).start()

    for piece in pieces:
        piece.start()
    for group in range(GROUPS):
        pltpu.make_async_copy(
            rows_ref.at[0:items], live_ref.at[items * group : items * (group + 1)], sems.at[group]
        ).wait()

        @pl.loop(items // 2 * group, items // 2 * (group + 1), unroll=True)
        def _(block):
            left = live_ref[2 * block]
            right = live_ref[2 * block + 1]
            for i in range(2):
                at = (block // 4) * 8 + block % 4 + 4 * i
                out_ref[at, :, 0:512] = left[:, 512 * i : 512 * (i + 1)]
                out_ref[at, :, 512:BASES] = right

    for piece in pieces:
        piece.wait()


def second_operand(facts, rows, keep, other):
    return pl.pallas_call(
        second_kernel,
        in_specs=[whole(pltpu.SMEM), whole(pl.ANY), whole(), whole()],
        out_specs=whole(),
        out_shape=pltpu.VMEM((CHIPS, SUB, BASES + 2 * WIDTH), jnp.bfloat16),
        scratch_shapes=[
            pltpu.VMEM((64, SUB, 1024), jnp.bfloat16),
            pltpu.SemaphoreType.DMA((GROUPS + 2,)),
        ],
        compiler_params=pltpu.CompilerParams(vmem_limit_bytes=8 * 2**20),
        cost_estimate=pl.CostEstimate(flops=0, bytes_accessed=8 * 10**6, transcendentals=0),
        name="second_operand",
    )(facts, rows, keep, other)


def third_kernel(facts_ref, got_ref, diagonal_ref, out_ref, sems):
    apart = pltpu.make_async_copy(
        diagonal_ref,
        out_ref.at[facts_ref[facts_ref[MINE]] // 2, :, 4 * WIDTH : 4 * WIDTH + 128],
        sems.at[0],
    )
    apart.start()

    @pl.loop(0, 32, unroll=True)
    def _(block):
        for side in range(2):
            code = facts_ref[2 * block + side]
            for half in range(2):
                source = (block // 4) * 8 + block % 4 + 4 * half
                lane = pl.multiple_of(code % 2 * (2 * WIDTH) + half * WIDTH, WIDTH)
                pltpu.make_async_copy(
                    got_ref.at[source, :, BASES + side * WIDTH : BASES + (side + 1) * WIDTH],
                    out_ref.at[code // 2, :, pl.ds(lane, WIDTH)],
                    sems.at[1],
                ).start()

    pltpu.make_async_copy(
        got_ref.at[:, :, BASES:], out_ref.at[0:CHIPS, :, 0 : 2 * WIDTH], sems.at[1]
    ).wait()
    apart.wait()


def third_operand(facts, got, diagonal):
    return pl.pallas_call(
        third_kernel,
        in_specs=[whole(pltpu.SMEM), whole(pl.ANY), whole(pl.ANY)],
        out_specs=whole(pl.ANY),
        out_shape=pltpu.HBM((128, SUB, 4 * WIDTH + 128), jnp.bfloat16),
        scratch_shapes=[pltpu.SemaphoreType.DMA((2,))],
        compiler_params=pltpu.CompilerParams(vmem_limit_bytes=8 * 2**20),
        cost_estimate=pl.CostEstimate(flops=0, bytes_accessed=4 * 10**6, transcendentals=0),
        name="third_operand",
    )(facts, pltpu.with_memory_space_constraint(got, pltpu.VMEM), diagonal)


def rotate_kernel(
    place_ref,
    block_ref,
    mine_ref,
    theirs_ref,
    first_ref,
    second_ref,
    new_first_ref,
    new_second_ref,
    direction_ref,
    held_ref,
    left_ref,
    right_ref,
    moment_ref,
    sems,
):
    col = place_ref[1]

    def load(source, target, n):
        return pltpu.make_async_copy(source, target, sems.at[n])

    lane = pl.multiple_of(512 + 512 * col, 512)
    lefts = []
    rights = []
    for n, source in enumerate((mine_ref, theirs_ref)):
        lefts.append(load(source.at[:, :, 0:512], left_ref.at[:, col ^ n], n))
        rights.append(load(source.at[:, :, pl.ds(lane, 512)], right_ref.at[:, col ^ n], 14 + n))
    for copy in lefts + rights:
        copy.start()
    load_block = load(block_ref, held_ref, 3)
    load_block.start()
    moments = [load(first_ref, moment_ref.at[0], 4), load(second_ref, moment_ref.at[1], 5)]
    for moment in moments:
        moment.start()
    for copy in lefts:
        copy.wait()
    load_block.wait()
    size = held_ref.shape[0]
    left_rot = dot_tn(left_ref[...].reshape(size, 512), held_ref[...]).astype(jnp.bfloat16)
    for copy in rights:
        copy.wait()
    for moment in moments:
        moment.wait()
    right = right_ref[...].reshape(size, 512)
    stores = []
    for part in range(4):
        rows = slice(128 * part, 128 * (part + 1))
        rotated = dot_nn(left_rot[rows], right)
        new_first = beta_one * moment_ref[0, rows] + (1.0 - beta_one) * rotated
        new_second = beta_two * moment_ref[1, rows] + (1.0 - beta_two) * rotated * rotated
        direction_ref[rows] = (new_first / (jnp.sqrt(new_second) + epsilon)).astype(jnp.bfloat16)
        moment_ref[0, rows] = new_first
        moment_ref[1, rows] = new_second
        for n, target in enumerate((new_first_ref, new_second_ref)):
            store = load(moment_ref.at[n, rows], target.at[rows], 6 + 2 * part + n)
            store.start()
            stores.append(store)
    for store in stores:
        store.wait()


def rotate(place, block, mine, theirs, first, second):
    half = first.shape[0]
    block, first, second = (
        pltpu.with_memory_space_constraint(value, pltpu.HBM) for value in (block, first, second)
    )
    return pl.pallas_call(
        rotate_kernel,
        in_specs=[whole(pltpu.SMEM)] + [whole(pl.ANY)] * 5,
        out_specs=[whole(pl.ANY), whole(pl.ANY), whole()],
        out_shape=[
            jax.ShapeDtypeStruct((half, half), jnp.float32),
            jax.ShapeDtypeStruct((half, half), jnp.float32),
            jax.ShapeDtypeStruct((half, half), jnp.bfloat16),
        ],
        scratch_shapes=[
            pltpu.VMEM((1024, 1024), jnp.bfloat16),
            pltpu.VMEM((CHIPS, 2, SUB, 512), jnp.bfloat16),
            pltpu.VMEM((CHIPS, 2, SUB, 512), jnp.bfloat16),
            pltpu.VMEM((2, half, half), jnp.float32),
            pltpu.SemaphoreType.DMA((16,)),
        ],
        compiler_params=pltpu.CompilerParams(vmem_limit_bytes=20 * 2**20),
        cost_estimate=pl.CostEstimate(
            flops=16 * 10**8, bytes_accessed=10**7, transcendentals=10**6
        ),
        name="rotate",
    )(place, block, mine, theirs, first, second)


def back_kernel(
    place_ref,
    own_ref,
    side_ref,
    mine_ref,
    theirs_ref,
    keep_ref,
    give_ref,
    left_ref,
    right_ref,
    strip_ref,
    sems,
):
    row = place_ref[0]
    col = place_ref[1]
    half = own_ref.shape[0]
    span = pl.ds(col * (CHIPS // 2), CHIPS // 2)
    lefts = []
    rights = []
    for n, source in enumerate((mine_ref, theirs_ref)):
        lefts.append(
            pltpu.make_async_copy(
                source.at[:, :, 0:512], left_ref.at[:, col ^ n], sems.at[n]
            )
        )
        rights.append(
            pltpu.make_async_copy(
                source.at[span, :, 512:BASES], right_ref.at[:, col ^ n], sems.at[2 + n]
            )
        )
    for copy in rights + lefts:
        copy.start()
    strip_ref[:, pl.ds(pl.multiple_of(col * half, half), half)] = own_ref[...]
    strip_ref[:, pl.ds(pl.multiple_of((1 - col) * half, half), half)] = side_ref[...]
    for copy in rights:
        copy.wait()
    half_back = dot_nt(strip_ref[...], right_ref[...].reshape(half, 1024)).astype(jnp.bfloat16)
    for copy in lefts:
        copy.wait()
    keep = left_ref[pl.ds(row * (CHIPS // 2), CHIPS // 2)].reshape(half, 512)
    give = left_ref[pl.ds((1 - row) * (CHIPS // 2), CHIPS // 2)].reshape(half, 512)
    give_ref[...] = dot_nn(give, half_back).astype(jnp.bfloat16)
    keep_ref[...] = dot_nn(keep, half_back)


def back(place, own, side, mine, theirs):
    half = own.shape[0]
    return pl.pallas_call(
        back_kernel,
        in_specs=[whole(pltpu.SMEM), whole(), whole(), whole(pl.ANY), whole(pl.ANY)],
        out_specs=[whole()] * 2,
        out_shape=[
            jax.ShapeDtypeStruct((half, half), jnp.float32),
            jax.ShapeDtypeStruct((half, half), jnp.bfloat16),
        ],
        scratch_shapes=[
            pltpu.VMEM((CHIPS, 2, SUB, 512), jnp.bfloat16),
            pltpu.VMEM((CHIPS // 2, 2, SUB, 1024), jnp.bfloat16),
            pltpu.VMEM((half, 2 * half), jnp.bfloat16),
            pltpu.SemaphoreType.DMA((4,)),
        ],
        compiler_params=PARAMS,
        cost_estimate=pl.CostEstimate(
            flops=11 * 10**8, bytes_accessed=6 * 10**6, transcendentals=0
        ),
        name="back",
    )(place, own, side, mine, theirs)


def settle_kernel(factor_ref, out_ref, strips_ref, sems):
    count = strips_ref.shape[0]
    loads = [
        pltpu.make_async_copy(factor_ref.at[strip_of(n)], strips_ref.at[n], sems.at[0, n])
        for n in range(count)
    ]
    stores = [
        pltpu.make_async_copy(strips_ref.at[n], out_ref.at[strip_of(n)], sems.at[1, n])
        for n in range(count)
    ]
    for load in loads:
        load.start()
    for load, store in zip(loads, stores):
        load.wait()
        store.start()
    for store in stores:
        store.wait()


def settle(factors):
    slots, size, _ = factors.shape
    return pl.pallas_call(
        settle_kernel,
        in_specs=[whole(pl.ANY)],
        out_specs=whole(pl.ANY),
        out_shape=pltpu.HBM(factors.shape, factors.dtype),
        scratch_shapes=[
            pltpu.VMEM((4 * slots, GB, size), jnp.float32),
            pltpu.SemaphoreType.DMA((2, 4 * slots)),
        ],
        compiler_params=pltpu.CompilerParams(vmem_limit_bytes=12 * 2**20),
        cost_estimate=pl.CostEstimate(
            flops=0, bytes_accessed=16 * 10**6, transcendentals=0
        ),
        name="settle",
    )(pltpu.with_memory_space_constraint(factors, pltpu.HBM))


def strip_of(n):
    return (n // 4, slice(GB * (n % 4), GB * (n % 4 + 1)))


def factor_kernel(
    facts_ref, factor_ref, got_ref, out_ref, strips_ref, held_ref, sems
):
    slots = factor_ref.shape[0]
    count = 4 * slots
    spans = [slice(2 * WIDTH * slot, 2 * WIDTH * (slot + 1)) for slot in range(slots)]
    spans.append(slice(2 * WIDTH * slots, got_ref.shape[3]))
    pieces = [
        pltpu.make_async_copy(
            got_ref.at[:, :, :, span], held_ref.at[:, :, :, span], sems.at[2 * count + n]
        )
        for n, span in enumerate(spans)
    ]
    loads = [
        pltpu.make_async_copy(out_ref.at[strip_of(n)], strips_ref.at[n], sems.at[n])
        for n in range(count)
    ]
    stores = [
        pltpu.make_async_copy(strips_ref.at[n], out_ref.at[strip_of(n)], sems.at[count + n])
        for n in range(count)
    ]
    for slot in range(slots):

        @pl.when(facts_ref[LIVE + slot] != 0)
        def _(slot=slot):
            pieces[slot].start()
            if slot == 0:
                pieces[slots].start()
            for n in range(4 * slot, 4 * (slot + 1)):
                loads[n].start()

    def piece(slot, which, n):
        lane = 2 * WIDTH * slot + (2 * which + n % 2) * 128
        halves = [
            held_ref[:, 2 * h + n // 2, :, lane : lane + 128]
            .astype(jnp.float32)
            .reshape(GB, 128)
            for h in range(2)
        ]
        return jnp.concatenate(halves, axis=1)

    def sub_block(slot, row, col):
        if row != col:
            pair = (min(row, col), max(row, col))
            which = 0 if pair in ABOVE[0] else 1
            value = piece(slot, which, ABOVE[which].index(pair))
            return value if row < col else value.T
        value = piece(slot, row // 2, 3)
        r, c = grid_positions()
        if row % 2 == 0:
            return jnp.where(r <= c, value, value.T)
        item = facts_ref[NAMED + slot]
        block = item // 2
        source = (block // 4 * 2 + row // 2) * 8 + block % 4 * 2 + item % 2
        tile = held_ref[source // 4, source % 4, :, 4 * WIDTH :].astype(jnp.float32)
        diagonal = jnp.concatenate([tile[0:1], tile[1:2]], axis=1)
        return jnp.where(r > c, value, jnp.where(r < c, value.T, diagonal))

    def mix(n):
        slot, row = n // 4, n % 4
        for col in range(4):
            span = slice(col * GB, (col + 1) * GB)
            strips_ref[n, :, span] = shampoo_beta * strips_ref[n, :, span] + (
                1.0 - shampoo_beta
            ) * sub_block(slot, row, col)

    for n in range(count):

        @pl.when(facts_ref[LIVE + n // 4] != 0)
        def _(n=n):
            if n % 4 == 0:
                pieces[n // 4].wait()
            if n == 0:
                pieces[slots].wait()
            loads[n].wait()
            mix(n)
            stores[n].start()

    for n in range(count):
        pl.when(facts_ref[LIVE + n // 4] != 0)(stores[n].wait)


def update_factors(facts, factors, got):
    slots, size, _ = factors.shape
    got = got.reshape(32, 4, SUB, got.shape[2])
    return pl.pallas_call(
        factor_kernel,
        in_specs=[whole(pltpu.SMEM)] + [whole(pl.ANY)] * 2,
        out_specs=whole(pl.ANY),
        out_shape=pltpu.HBM(factors.shape, factors.dtype),
        scratch_shapes=[
            pltpu.VMEM((4 * slots, GB, size), jnp.float32),
            pltpu.VMEM(got.shape, got.dtype),
            pltpu.SemaphoreType.DMA((9 * slots + 1,)),
        ],
        input_output_aliases={1: 0},
        compiler_params=pltpu.CompilerParams(vmem_limit_bytes=20 * 2**20),
        cost_estimate=pl.CostEstimate(
            flops=4 * 10**6, bytes_accessed=2 * 10**7, transcendentals=0
        ),
        name="update_factors",
    )(facts, pltpu.with_memory_space_constraint(factors, pltpu.HBM), got)


def shards(gradient, first_moment, second_moment, factors, eigen_bases, owners):
    devices = lax.axis_size("fsdp") * lax.axis_size("rep")
    slots = factors.shape[0]
    size = factors.shape[1]
    item_count = owners.shape[0]
    fsdp_index = lax.axis_index("fsdp")
    rep_index = lax.axis_index("rep")
    my_index = fsdp_index * lax.axis_size("rep") + rep_index
    my_item = (fsdp_index // 2 * 8 + rep_index).reshape(1).astype(jnp.int32)
    place = jnp.stack([fsdp_index % 2, rep_index % 2]).astype(jnp.int32)

    below = swap_neighbour(gradient, "fsdp")
    first_parts = interleave(eigen_bases, devices)
    first_got = lax.all_to_all(first_parts, BOTH, 0, 0, tiled=True)

    item_index = jnp.arange(item_count, dtype=jnp.int32)
    earlier_same = (owners[:, None] == owners[None, :]) & (
        item_index[None, :] < item_index[:, None]
    )
    codes = slots * owners + jnp.sum(earlier_same.astype(jnp.int32), axis=1)
    my_codes = my_index * slots + jnp.arange(slots, dtype=jnp.int32)
    hits = (codes[None, :] == my_codes[:, None]).astype(jnp.int32)
    live = jnp.sum(hits, axis=1)
    items = jnp.sum(hits * item_index[None, :], axis=1)
    facts = jnp.concatenate([codes, place, my_item, live, items]).astype(jnp.int32)

    side = swap_neighbour(gradient, "rep")
    cross = swap_neighbour(below, "rep")
    quads = (gradient, side, below, cross)
    settled = settle(factors)
    kept_gram, given_gram, diagonal, block = gram_pieces(place, quads)
    other_gram = swap_neighbour(given_gram.reshape(CHIPS, SUB, WIDTH), "rep")
    kept_gram = kept_gram.reshape(CHIPS, SUB, WIDTH)

    second_parts = second_operand(
        facts, first_got.reshape(devices * slots, SUB, size), kept_gram, other_gram
    )
    same_core = [[2 * chip + core for chip in range(CHIPS)] for core in range(2)]
    mine = lax.all_to_all(
        second_parts, BOTH, 0, 0, axis_index_groups=same_core, tiled=True
    )
    theirs = swap_neighbour(mine, "rep")

    third_parts = third_operand(facts, mine, diagonal)
    third_got = lax.all_to_all(third_parts, BOTH, 0, 0, tiled=True)

    new_first, new_second, direction = rotate(
        place, block, mine, theirs, first_moment, second_moment
    )
    other = swap_neighbour(direction, "rep")
    keep, give = back(place, direction, other, mine, theirs)
    update = keep + swap_neighbour(give, "fsdp").astype(jnp.float32)
    new_factors = update_factors(facts, settled, third_got)
    return (update, new_first, new_second, new_factors)


def solution(mesh):
    in_specs = (
        P("fsdp", "rep"),
        P("fsdp", "rep"),
        P("fsdp", "rep"),
        P(("fsdp", "rep"), None, None),
        P(("fsdp", "rep"), None, None),
        P(),
    )
    out_specs = (
        P("fsdp", "rep"),
        P("fsdp", "rep"),
        P("fsdp", "rep"),
        P(("fsdp", "rep"), None, None),
    )
    return jax.shard_map(shards, mesh=mesh, in_specs=in_specs, out_specs=out_specs, check_vma=False)
```

```python
import functools

import jax
import jax.numpy as jnp
from jax import lax
from jax.experimental import pallas as pl
from jax.experimental.pallas import tpu as pltpu
from jax.sharding import PartitionSpec as P

beta_one = 0.9
beta_two = 0.95
shampoo_beta = 0.95
epsilon = 1e-08

SUB = 8
GB = 256
ABOVE = (((0, 1), (0, 2), (0, 3)), ((1, 2), (1, 3), (2, 3)))
WIDTH = 2 * 128
CHIPS = 64
ROW, COL, MINE, LIVE, NAMED = 64, 65, 66, 67, 69
BASES = 512 + 1024
SPARE = BASES + 2 * WIDTH
BOTH = ("fsdp", "rep")
PARAMS = pltpu.CompilerParams(vmem_limit_bytes=24 * 2**20)


def swap_neighbour(value, axis):
    pairs = [(source, source ^ 1) for source in range(lax.axis_size(axis))]
    return lax.ppermute(value, axis, pairs)


def dot_nn(left, right):
    return jnp.dot(left, right, preferred_element_type=jnp.float32)


def dot_tn(left, right):
    return lax.dot_general(
        left, right, (((0,), (0,)), ((), ())), preferred_element_type=jnp.float32
    )


def dot_nt(left, right):
    return lax.dot_general(
        left, right, (((1,), (1,)), ((), ())), preferred_element_type=jnp.float32
    )


def whole(memory_space=pltpu.VMEM):
    return pl.BlockSpec(memory_space=memory_space)


def interleave_kernel(src_ref, dst_ref, held_ref, sems):
    slots, devices = held_ref.shape[0], held_ref.shape[1]
    stores = []
    loads = []
    for n in range(2 * slots):
        slot, span = n % slots, pl.ds(n // slots * (devices // 2), devices // 2)
        held = held_ref.at[slot, span]
        loads.append(pltpu.make_async_copy(src_ref.at[slot, span], held, sems.at[0, n]))
        stores.append(pltpu.make_async_copy(held, dst_ref.at[span, slot], sems.at[1, n]))
        loads[n].start()
    for load, store in zip(loads, stores):
        load.wait()
        store.start()
    for store in stores:
        store.wait()


def interleave(bases, devices):
    slots, size, _ = bases.shape
    parts = bases.reshape(slots, devices, SUB, size)
    return pl.pallas_call(
        interleave_kernel,
        in_specs=[whole(pl.ANY)],
        out_specs=whole(pl.ANY),
        out_shape=pltpu.HBM((devices, slots, SUB, size), bases.dtype),
        scratch_shapes=[
            pltpu.VMEM(parts.shape, bases.dtype),
            pltpu.SemaphoreType.DMA((2, 2 * slots)),
        ],
        compiler_params=pltpu.CompilerParams(vmem_limit_bytes=8 * 2**20),
        cost_estimate=pl.CostEstimate(flops=0, bytes_accessed=8 * 10**6, transcendentals=0),
        name="interleave",
    )(pltpu.with_memory_space_constraint(parts, pltpu.HBM))


def place_quads(row, col, quads, block_ref):
    half = quads[0].shape[0]
    for dr in range(2):
        for dc in range(2):
            at = (pl.multiple_of((row ^ dr) * half, half), pl.multiple_of((col ^ dc) * half, half))
            block_ref[pl.ds(at[0], half), pl.ds(at[1], half)] = quads[2 * dr + dc][...]


def grid_positions():
    shape = (GB, GB)
    return lax.broadcasted_iota(jnp.int32, shape, 0), lax.broadcasted_iota(jnp.int32, shape, 1)


def gram_kernel(
    place_ref, own_ref, side_ref, below_ref, cross_ref, keep_ref, give_ref, diagonal_ref, block_ref
):
    row = place_ref[0]
    col = place_ref[1]
    place_quads(row, col, (own_ref, side_ref, below_ref, cross_ref), block_ref)

    def emit(left_gram, which):
        def product(first, second):
            a = slice(first * GB, (first + 1) * GB)
            b = slice(second * GB, (second + 1) * GB)
            if left_gram:
                return dot_nt(block_ref[a, :], block_ref[b, :])
            return dot_tn(block_ref[:, a], block_ref[:, b])

        r, c = grid_positions()
        upper = product(2 * which, 2 * which)
        lower = product(2 * which + 1, 2 * which + 1)
        diagonal = jnp.sum(jnp.where(r == c, lower, 0.0), axis=0, keepdims=True)
        tile_row = lax.broadcasted_iota(jnp.int32, (SUB, 128), 0)
        diagonal_ref[...] = jnp.where(
            tile_row == 0, diagonal[:, :128], jnp.where(tile_row == 1, diagonal[:, 128:], 0.0)
        ).astype(jnp.bfloat16)
        for n in range(4):
            if n < 3:
                value = product(*ABOVE[which][n])
            else:
                value = jnp.where(r <= c, upper, lower)
            for half in range(2):
                tiles = value[:, half * 128 : (half + 1) * 128].reshape(GB // SUB, SUB, 128)
                span = slice(n % 2 * 128, (n % 2 + 1) * 128)
                kept = n // 2 == (0 if left_gram else 1)
                target = keep_ref if kept else give_ref
                target[:, half, :, span] = tiles.astype(jnp.bfloat16)

    for left_gram in (True, False):
        for which in range(2):
            pl.when((col == (0 if left_gram else 1)) & (row == which))(
                functools.partial(emit, left_gram, which)
            )


def gram_pieces(place, quads):
    size = 2 * quads[0].shape[0]
    return pl.pallas_call(
        gram_kernel,
        in_specs=[whole(pltpu.SMEM)] + [whole()] * 4,
        out_specs=[whole()] * 4,
        out_shape=[
            jax.ShapeDtypeStruct((32, 2, SUB, WIDTH), jnp.bfloat16),
            jax.ShapeDtypeStruct((32, 2, SUB, WIDTH), jnp.bfloat16),
            jax.ShapeDtypeStruct((SUB, 128), jnp.bfloat16),
            pltpu.HBM((size, size), jnp.bfloat16),
        ],
        compiler_params=PARAMS,
        cost_estimate=pl.CostEstimate(
            flops=32 * 10**9, bytes_accessed=3 * 10**6, transcendentals=0
        ),
        name="gram_pieces",
    )(place, *quads)


GROUPS = 4


def second_kernel(
    facts_ref, rows_ref, keep_ref, other_ref, diagonal_ref, out_ref, live_ref, sems
):
    core = facts_ref[COL]
    items = live_ref.shape[0] // GROUPS
    pieces = []
    for n, source in enumerate((keep_ref, other_ref)):
        lane = pl.multiple_of(BASES + WIDTH * (core ^ n), WIDTH)
        pieces.append(
            pltpu.make_async_copy(
                source, out_ref.at[:, :, pl.ds(lane, WIDTH)], sems.at[GROUPS + n]
            )
        )
    owner = facts_ref[facts_ref[MINE]] // 4
    pieces.append(
        pltpu.make_async_copy(
            diagonal_ref, out_ref.at[owner, :, SPARE : SPARE + 128], sems.at[GROUPS + 2]
        )
    )
    for group in range(GROUPS):

        @pl.loop(items * group, items * (group + 1), unroll=True)
        def _(item, group=group):
            pltpu.make_async_copy(
                rows_ref.at[facts_ref[item]], live_ref.at[item], sems.at[group]
            ).start()

    for piece in pieces:
        piece.start()
    for group in range(GROUPS):
        pltpu.make_async_copy(
            rows_ref.at[0:items], live_ref.at[items * group : items * (group + 1)], sems.at[group]
        ).wait()

        @pl.loop(items // 2 * group, items // 2 * (group + 1), unroll=True)
        def _(block):
            left = live_ref[2 * block]
            right = live_ref[2 * block + 1]
            for i in range(2):
                at = (block // 4) * 8 + block % 4 + 4 * i
                out_ref[at, :, 0:512] = left[:, 512 * i : 512 * (i + 1)]
                out_ref[at, :, 512:BASES] = right

    for piece in pieces:
        piece.wait()


def second_operand(facts, rows, keep, other, diagonal):
    return pl.pallas_call(
        second_kernel,
        in_specs=[whole(pltpu.SMEM), whole(pl.ANY), whole(), whole(), whole()],
        out_specs=whole(),
        out_shape=pltpu.VMEM((CHIPS, SUB, SPARE + 128), jnp.bfloat16),
        scratch_shapes=[
            pltpu.VMEM((64, SUB, 1024), jnp.bfloat16),
            pltpu.SemaphoreType.DMA((GROUPS + 3,)),
        ],
        compiler_params=pltpu.CompilerParams(vmem_limit_bytes=8 * 2**20),
        cost_estimate=pl.CostEstimate(flops=0, bytes_accessed=8 * 10**6, transcendentals=0),
        name="second_operand",
    )(facts, rows, keep, other, diagonal)


def third_kernel(facts_ref, got_ref, out_ref, sems):
    @pl.loop(0, 32, unroll=True)
    def _(block):
        for side in range(2):
            code = facts_ref[2 * block + side]
            for half in range(2):
                source = (block // 4) * 8 + block % 4 + 4 * half
                lane = pl.multiple_of(code % 2 * (2 * WIDTH) + half * WIDTH, WIDTH)
                pltpu.make_async_copy(
                    got_ref.at[source, :, BASES + side * WIDTH : BASES + (side + 1) * WIDTH],
                    out_ref.at[code // 2, :, pl.ds(lane, WIDTH)],
                    sems.at[0],
                ).start()

    pltpu.make_async_copy(
        got_ref.at[:, :, BASES:SPARE], out_ref.at[0:CHIPS, :, 0 : 2 * WIDTH], sems.at[0]
    ).wait()


def third_operand(facts, got):
    return pl.pallas_call(
        third_kernel,
        in_specs=[whole(pltpu.SMEM), whole(pl.ANY)],
        out_specs=whole(pl.ANY),
        out_shape=pltpu.HBM((128, SUB, 4 * WIDTH), jnp.bfloat16),
        scratch_shapes=[pltpu.SemaphoreType.DMA((1,))],
        compiler_params=pltpu.CompilerParams(vmem_limit_bytes=8 * 2**20),
        cost_estimate=pl.CostEstimate(flops=0, bytes_accessed=4 * 10**6, transcendentals=0),
        name="third_operand",
    )(facts, pltpu.with_memory_space_constraint(got, pltpu.VMEM))


def rotate_kernel(
    facts_ref,
    block_ref,
    mine_ref,
    theirs_ref,
    first_ref,
    second_ref,
    new_first_ref,
    new_second_ref,
    direction_ref,
    spare_ref,
    held_ref,
    left_ref,
    right_ref,
    moment_ref,
    sems,
):
    col = facts_ref[COL]

    def load(source, target, n):
        return pltpu.make_async_copy(source, target, sems.at[n])

    def spare(source, n):
        item = facts_ref[NAMED + n // 2]
        block = item // 2
        chip = (block // 4 * 2 + n % 2) * 4 + block % 4
        return load(source.at[chip, :, SPARE : SPARE + 128], spare_ref.at[n], 16 + n)

    for n in range(4):
        same = facts_ref[NAMED + n // 2] % 2 == col
        pl.when(same)(spare(mine_ref, n).start)
        pl.when(jnp.logical_not(same))(spare(theirs_ref, n).start)

    lane = pl.multiple_of(512 + 512 * col, 512)
    lefts = []
    rights = []
    for n, source in enumerate((mine_ref, theirs_ref)):
        lefts.append(load(source.at[:, :, 0:512], left_ref.at[:, col ^ n], n))
        rights.append(load(source.at[:, :, pl.ds(lane, 512)], right_ref.at[:, col ^ n], 14 + n))
    for copy in lefts + rights:
        copy.start()
    load_block = load(block_ref, held_ref, 3)
    load_block.start()
    moments = [load(first_ref, moment_ref.at[0], 4), load(second_ref, moment_ref.at[1], 5)]
    for moment in moments:
        moment.start()
    for copy in lefts:
        copy.wait()
    load_block.wait()
    size = held_ref.shape[0]
    left_rot = dot_tn(left_ref[...].reshape(size, 512), held_ref[...]).astype(jnp.bfloat16)
    for copy in rights:
        copy.wait()
    for moment in moments:
        moment.wait()
    right = right_ref[...].reshape(size, 512)
    stores = []
    for part in range(4):
        rows = slice(128 * part, 128 * (part + 1))
        rotated = dot_nn(left_rot[rows], right)
        new_first = beta_one * moment_ref[0, rows] + (1.0 - beta_one) * rotated
        new_second = beta_two * moment_ref[1, rows] + (1.0 - beta_two) * rotated * rotated
        direction_ref[rows] = (new_first / (jnp.sqrt(new_second) + epsilon)).astype(jnp.bfloat16)
        moment_ref[0, rows] = new_first
        moment_ref[1, rows] = new_second
        for n, target in enumerate((new_first_ref, new_second_ref)):
            store = load(moment_ref.at[n, rows], target.at[rows], 6 + 2 * part + n)
            store.start()
            stores.append(store)
    for store in stores:
        store.wait()
    for n in range(4):
        spare(mine_ref, n).wait()


def rotate(facts, block, mine, theirs, first, second):
    half = first.shape[0]
    block, first, second = (
        pltpu.with_memory_space_constraint(value, pltpu.HBM) for value in (block, first, second)
    )
    return pl.pallas_call(
        rotate_kernel,
        in_specs=[whole(pltpu.SMEM)] + [whole(pl.ANY)] * 5,
        out_specs=[whole(pl.ANY), whole(pl.ANY), whole(), whole(pl.ANY)],
        out_shape=[
            jax.ShapeDtypeStruct((half, half), jnp.float32),
            jax.ShapeDtypeStruct((half, half), jnp.float32),
            jax.ShapeDtypeStruct((half, half), jnp.bfloat16),
            pltpu.HBM((4, SUB, 128), jnp.bfloat16),
        ],
        scratch_shapes=[
            pltpu.VMEM((1024, 1024), jnp.bfloat16),
            pltpu.VMEM((CHIPS, 2, SUB, 512), jnp.bfloat16),
            pltpu.VMEM((CHIPS, 2, SUB, 512), jnp.bfloat16),
            pltpu.VMEM((2, half, half), jnp.float32),
            pltpu.SemaphoreType.DMA((20,)),
        ],
        compiler_params=pltpu.CompilerParams(vmem_limit_bytes=20 * 2**20),
        cost_estimate=pl.CostEstimate(
            flops=16 * 10**8, bytes_accessed=10**7, transcendentals=10**6
        ),
        name="rotate",
    )(facts, block, mine, theirs, first, second)


def back_kernel(
    place_ref,
    own_ref,
    side_ref,
    mine_ref,
    theirs_ref,
    keep_ref,
    give_ref,
    left_ref,
    right_ref,
    strip_ref,
    sems,
):
    row = place_ref[0]
    col = place_ref[1]
    half = own_ref.shape[0]
    span = pl.ds(col * (CHIPS // 2), CHIPS // 2)
    lefts = []
    rights = []
    for n, source in enumerate((mine_ref, theirs_ref)):
        lefts.append(
            pltpu.make_async_copy(
                source.at[:, :, 0:512], left_ref.at[:, col ^ n], sems.at[n]
            )
        )
        rights.append(
            pltpu.make_async_copy(
                source.at[span, :, 512:BASES], right_ref.at[:, col ^ n], sems.at[2 + n]
            )
        )
    for copy in rights + lefts:
        copy.start()
    strip_ref[:, pl.ds(pl.multiple_of(col * half, half), half)] = own_ref[...]
    strip_ref[:, pl.ds(pl.multiple_of((1 - col) * half, half), half)] = side_ref[...]
    for copy in rights:
        copy.wait()
    half_back = dot_nt(strip_ref[...], right_ref[...].reshape(half, 1024)).astype(jnp.bfloat16)
    for copy in lefts:
        copy.wait()
    keep = left_ref[pl.ds(row * (CHIPS // 2), CHIPS // 2)].reshape(half, 512)
    give = left_ref[pl.ds((1 - row) * (CHIPS // 2), CHIPS // 2)].reshape(half, 512)
    give_ref[...] = dot_nn(give, half_back).astype(jnp.bfloat16)
    keep_ref[...] = dot_nn(keep, half_back)


def back(place, own, side, mine, theirs):
    half = own.shape[0]
    return pl.pallas_call(
        back_kernel,
        in_specs=[whole(pltpu.SMEM), whole(), whole(), whole(pl.ANY), whole(pl.ANY)],
        out_specs=[whole()] * 2,
        out_shape=[
            jax.ShapeDtypeStruct((half, half), jnp.float32),
            jax.ShapeDtypeStruct((half, half), jnp.bfloat16),
        ],
        scratch_shapes=[
            pltpu.VMEM((CHIPS, 2, SUB, 512), jnp.bfloat16),
            pltpu.VMEM((CHIPS // 2, 2, SUB, 1024), jnp.bfloat16),
            pltpu.VMEM((half, 2 * half), jnp.bfloat16),
            pltpu.SemaphoreType.DMA((4,)),
        ],
        compiler_params=PARAMS,
        cost_estimate=pl.CostEstimate(
            flops=11 * 10**8, bytes_accessed=6 * 10**6, transcendentals=0
        ),
        name="back",
    )(place, own, side, mine, theirs)


def finish_kernel(keep_ref, other_ref, out_ref, sum_ref, sems):
    parts = sems.shape[0]
    rows = sum_ref.shape[0] // parts
    stores = []
    for part in range(parts):
        span = slice(rows * part, rows * (part + 1))
        sum_ref[span] = keep_ref[span] + other_ref[span].astype(jnp.float32)
        stores.append(pltpu.make_async_copy(sum_ref.at[span], out_ref.at[span], sems.at[part]))
        stores[part].start()
    for store in stores:
        store.wait()


def finish(keep, other):
    keep, other = (
        pltpu.with_memory_space_constraint(value, pltpu.VMEM) for value in (keep, other)
    )
    return pl.pallas_call(
        finish_kernel,
        in_specs=[whole()] * 2,
        out_specs=whole(pl.ANY),
        out_shape=pltpu.HBM(keep.shape, keep.dtype),
        scratch_shapes=[
            pltpu.VMEM(keep.shape, keep.dtype),
            pltpu.SemaphoreType.DMA((4,)),
        ],
        compiler_params=pltpu.CompilerParams(vmem_limit_bytes=8 * 2**20),
        cost_estimate=pl.CostEstimate(
            flops=3 * 10**5, bytes_accessed=2 * 10**6, transcendentals=0
        ),
        name="finish",
    )(keep, other)


def settle_kernel(factor_ref, out_ref, strips_ref, sems):
    count = strips_ref.shape[0]
    loads = [
        pltpu.make_async_copy(factor_ref.at[strip_of(n)], strips_ref.at[n], sems.at[0, n])
        for n in range(count)
    ]
    stores = [
        pltpu.make_async_copy(strips_ref.at[n], out_ref.at[strip_of(n)], sems.at[1, n])
        for n in range(count)
    ]
    for load in loads:
        load.start()
    for load, store in zip(loads, stores):
        load.wait()
        store.start()
    for store in stores:
        store.wait()


def settle(factors):
    slots, size, _ = factors.shape
    return pl.pallas_call(
        settle_kernel,
        in_specs=[whole(pl.ANY)],
        out_specs=whole(pl.ANY),
        out_shape=pltpu.HBM(factors.shape, factors.dtype),
        scratch_shapes=[
            pltpu.VMEM((4 * slots, GB, size), jnp.float32),
            pltpu.SemaphoreType.DMA((2, 4 * slots)),
        ],
        compiler_params=pltpu.CompilerParams(vmem_limit_bytes=12 * 2**20),
        cost_estimate=pl.CostEstimate(
            flops=0, bytes_accessed=16 * 10**6, transcendentals=0
        ),
        name="settle",
    )(pltpu.with_memory_space_constraint(factors, pltpu.HBM))


def strip_of(n):
    return (n // 4, slice(GB * (n % 4), GB * (n % 4 + 1)))


def factor_kernel(
    facts_ref, factor_ref, got_ref, spare_ref, out_ref, strips_ref, held_ref, diagonal_ref, sems
):
    slots = factor_ref.shape[0]
    count = 4 * slots
    spans = [slice(2 * WIDTH * slot, 2 * WIDTH * (slot + 1)) for slot in range(slots)]
    pieces = [
        pltpu.make_async_copy(
            got_ref.at[:, :, :, span], held_ref.at[:, :, :, span], sems.at[2 * count + n]
        )
        for n, span in enumerate(spans)
    ]
    loads = [
        pltpu.make_async_copy(out_ref.at[strip_of(n)], strips_ref.at[n], sems.at[n])
        for n in range(count)
    ]
    stores = [
        pltpu.make_async_copy(strips_ref.at[n], out_ref.at[strip_of(n)], sems.at[count + n])
        for n in range(count)
    ]
    diagonals = pltpu.make_async_copy(spare_ref, diagonal_ref, sems.at[9 * slots])
    diagonals.start()
    for slot in range(slots):

        @pl.when(facts_ref[LIVE + slot] != 0)
        def _(slot=slot):
            pieces[slot].start()
            for n in range(4 * slot, 4 * (slot + 1)):
                loads[n].start()

    def piece(slot, which, n):
        lane = 2 * WIDTH * slot + (2 * which + n % 2) * 128
        halves = [
            held_ref[:, 2 * h + n // 2, :, lane : lane + 128]
            .astype(jnp.float32)
            .reshape(GB, 128)
            for h in range(2)
        ]
        return jnp.concatenate(halves, axis=1)

    def sub_block(slot, row, col):
        if row != col:
            pair = (min(row, col), max(row, col))
            which = 0 if pair in ABOVE[0] else 1
            value = piece(slot, which, ABOVE[which].index(pair))
            return value if row < col else value.T
        value = piece(slot, row // 2, 3)
        r, c = grid_positions()
        if row % 2 == 0:
            return jnp.where(r <= c, value, value.T)
        tile = diagonal_ref[2 * slot + row // 2].astype(jnp.float32)
        diagonal = jnp.concatenate([tile[0:1], tile[1:2]], axis=1)
        return jnp.where(r > c, value, jnp.where(r < c, value.T, diagonal))

    def mix(n):
        slot, row = n // 4, n % 4
        for col in range(4):
            span = slice(col * GB, (col + 1) * GB)
            strips_ref[n, :, span] = shampoo_beta * strips_ref[n, :, span] + (
                1.0 - shampoo_beta
            ) * sub_block(slot, row, col)

    diagonals.wait()
    for n in range(count):

        @pl.when(facts_ref[LIVE + n // 4] != 0)
        def _(n=n):
            if n % 4 == 0:
                pieces[n // 4].wait()
            loads[n].wait()
            mix(n)
            stores[n].start()

    for n in range(count):
        pl.when(facts_ref[LIVE + n // 4] != 0)(stores[n].wait)


def update_factors(facts, factors, got, spare):
    slots, size, _ = factors.shape
    got = got.reshape(32, 4, SUB, got.shape[2])
    return pl.pallas_call(
        factor_kernel,
        in_specs=[whole(pltpu.SMEM)] + [whole(pl.ANY)] * 3,
        out_specs=whole(pl.ANY),
        out_shape=pltpu.HBM(factors.shape, factors.dtype),
        scratch_shapes=[
            pltpu.VMEM((4 * slots, GB, size), jnp.float32),
            pltpu.VMEM(got.shape, got.dtype),
            pltpu.VMEM(spare.shape, spare.dtype),
            pltpu.SemaphoreType.DMA((9 * slots + 1,)),
        ],
        input_output_aliases={1: 0},
        compiler_params=pltpu.CompilerParams(vmem_limit_bytes=20 * 2**20),
        cost_estimate=pl.CostEstimate(
            flops=4 * 10**6, bytes_accessed=2 * 10**7, transcendentals=0
        ),
        name="update_factors",
    )(facts, pltpu.with_memory_space_constraint(factors, pltpu.HBM), got, spare)


def shards(gradient, first_moment, second_moment, factors, eigen_bases, owners):
    devices = lax.axis_size("fsdp") * lax.axis_size("rep")
    slots = factors.shape[0]
    size = factors.shape[1]
    item_count = owners.shape[0]
    fsdp_index = lax.axis_index("fsdp")
    rep_index = lax.axis_index("rep")
    my_index = fsdp_index * lax.axis_size("rep") + rep_index
    my_item = (fsdp_index // 2 * 8 + rep_index).reshape(1).astype(jnp.int32)
    place = jnp.stack([fsdp_index % 2, rep_index % 2]).astype(jnp.int32)

    below = swap_neighbour(gradient, "fsdp")
    first_parts = interleave(eigen_bases, devices)
    first_got = lax.all_to_all(first_parts, BOTH, 0, 0, tiled=True)

    item_index = jnp.arange(item_count, dtype=jnp.int32)
    earlier_same = (owners[:, None] == owners[None, :]) & (
        item_index[None, :] < item_index[:, None]
    )
    codes = slots * owners + jnp.sum(earlier_same.astype(jnp.int32), axis=1)
    my_codes = my_index * slots + jnp.arange(slots, dtype=jnp.int32)
    hits = (codes[None, :] == my_codes[:, None]).astype(jnp.int32)
    live = jnp.sum(hits, axis=1)
    items = jnp.sum(hits * item_index[None, :], axis=1)
    facts = jnp.concatenate([codes, place, my_item, live, items]).astype(jnp.int32)

    side = swap_neighbour(gradient, "rep")
    cross = swap_neighbour(below, "rep")
    quads = (gradient, side, below, cross)
    settled = settle(factors)
    kept_gram, given_gram, diagonal, block = gram_pieces(place, quads)
    other_gram = swap_neighbour(given_gram.reshape(CHIPS, SUB, WIDTH), "rep")
    kept_gram = kept_gram.reshape(CHIPS, SUB, WIDTH)

    second_parts = second_operand(
        facts, first_got.reshape(devices * slots, SUB, size), kept_gram, other_gram, diagonal
    )
    same_core = [[2 * chip + core for chip in range(CHIPS)] for core in range(2)]
    mine = lax.all_to_all(
        second_parts, BOTH, 0, 0, axis_index_groups=same_core, tiled=True
    )
    theirs = swap_neighbour(mine, "rep")

    third_parts = third_operand(facts, mine)
    third_got = lax.all_to_all(third_parts, BOTH, 0, 0, tiled=True)

    new_first, new_second, direction, spare = rotate(
        facts, block, mine, theirs, first_moment, second_moment
    )
    other = swap_neighbour(direction, "rep")
    keep, give = back(place, direction, other, mine, theirs)
    update = finish(keep, swap_neighbour(give, "fsdp"))
    new_factors = update_factors(facts, settled, third_got, spare)
    return (update, new_first, new_second, new_factors)


def solution(mesh):
    in_specs = (
        P("fsdp", "rep"),
        P("fsdp", "rep"),
        P("fsdp", "rep"),
        P(("fsdp", "rep"), None, None),
        P(("fsdp", "rep"), None, None),
        P(),
    )
    out_specs = (
        P("fsdp", "rep"),
        P("fsdp", "rep"),
        P("fsdp", "rep"),
        P(("fsdp", "rep"), None, None),
    )
    return jax.shard_map(shards, mesh=mesh, in_specs=in_specs, out_specs=out_specs, check_vma=False)
```

```python
import functools

import jax
import jax.numpy as jnp
from jax import lax
from jax.experimental import pallas as pl
from jax.experimental.pallas import tpu as pltpu
from jax.sharding import PartitionSpec as P

beta_one = 0.9
beta_two = 0.95
shampoo_beta = 0.95
epsilon = 1e-08

SUB = 8
GB = 256
ABOVE = (((0, 1), (0, 2), (0, 3)), ((1, 2), (1, 3), (2, 3)))
WIDTH = 2 * 128
CHIPS = 64
READY = 1
ROW, COL, MINE, LIVE, NAMED = 64, 65, 66, 67, 69
BASES = 512 + 1024
SPARE = BASES + 2 * WIDTH
BOTH = ("fsdp", "rep")
PARAMS = pltpu.CompilerParams(vmem_limit_bytes=24 * 2**20)


def swap_neighbour(value, axis):
    pairs = [(source, source ^ 1) for source in range(lax.axis_size(axis))]
    return lax.ppermute(value, axis, pairs)


def dot_nn(left, right):
    return jnp.dot(left, right, preferred_element_type=jnp.float32)


def dot_tn(left, right):
    return lax.dot_general(
        left, right, (((0,), (0,)), ((), ())), preferred_element_type=jnp.float32
    )


def dot_nt(left, right):
    return lax.dot_general(
        left, right, (((1,), (1,)), ((), ())), preferred_element_type=jnp.float32
    )


def whole(memory_space=pltpu.VMEM):
    return pl.BlockSpec(memory_space=memory_space)


def interleave_kernel(src_ref, dst_ref, held_ref, sems):
    slots, devices = held_ref.shape[0], held_ref.shape[1]
    stores = []
    loads = []
    for n in range(2 * slots):
        slot, span = n % slots, pl.ds(n // slots * (devices // 2), devices // 2)
        held = held_ref.at[slot, span]
        loads.append(pltpu.make_async_copy(src_ref.at[slot, span], held, sems.at[0, n]))
        stores.append(pltpu.make_async_copy(held, dst_ref.at[span, slot], sems.at[1, n]))
        loads[n].start()
    for load, store in zip(loads, stores):
        load.wait()
        store.start()
    for store in stores:
        store.wait()


def interleave(bases, devices):
    slots, size, _ = bases.shape
    parts = bases.reshape(slots, devices, SUB, size)
    return pl.pallas_call(
        interleave_kernel,
        in_specs=[whole(pl.ANY)],
        out_specs=whole(pl.ANY),
        out_shape=pltpu.HBM((devices, slots, SUB, size), bases.dtype),
        scratch_shapes=[
            pltpu.VMEM(parts.shape, bases.dtype),
            pltpu.SemaphoreType.DMA((2, 2 * slots)),
        ],
        compiler_params=pltpu.CompilerParams(vmem_limit_bytes=8 * 2**20),
        cost_estimate=pl.CostEstimate(flops=0, bytes_accessed=8 * 10**6, transcendentals=0),
        name="interleave",
    )(pltpu.with_memory_space_constraint(parts, pltpu.HBM))


def place_quads(row, col, quads, block_ref):
    half = quads[0].shape[0]
    for dr in range(2):
        for dc in range(2):
            at = (pl.multiple_of((row ^ dr) * half, half), pl.multiple_of((col ^ dc) * half, half))
            block_ref[pl.ds(at[0], half), pl.ds(at[1], half)] = quads[2 * dr + dc][...]


def grid_positions():
    shape = (GB, GB)
    return lax.broadcasted_iota(jnp.int32, shape, 0), lax.broadcasted_iota(jnp.int32, shape, 1)


def gram_kernel(
    place_ref, own_ref, side_ref, below_ref, cross_ref, keep_ref, give_ref, diagonal_ref, block_ref
):
    row = place_ref[0]
    col = place_ref[1]
    place_quads(row, col, (own_ref, side_ref, below_ref, cross_ref), block_ref)

    def emit(left_gram, which):
        def product(first, second):
            a = slice(first * GB, (first + 1) * GB)
            b = slice(second * GB, (second + 1) * GB)
            if left_gram:
                return dot_nt(block_ref[a, :], block_ref[b, :])
            return dot_tn(block_ref[:, a], block_ref[:, b])

        r, c = grid_positions()
        upper = product(2 * which, 2 * which)
        lower = product(2 * which + 1, 2 * which + 1)
        diagonal = jnp.sum(jnp.where(r == c, lower, 0.0), axis=0, keepdims=True)
        tile_row = lax.broadcasted_iota(jnp.int32, (SUB, 128), 0)
        diagonal_ref[...] = jnp.where(
            tile_row == 0, diagonal[:, :128], jnp.where(tile_row == 1, diagonal[:, 128:], 0.0)
        ).astype(jnp.bfloat16)
        for n in range(4):
            if n < 3:
                value = product(*ABOVE[which][n])
            else:
                value = jnp.where(r <= c, upper, lower)
            for half in range(2):
                tiles = value[:, half * 128 : (half + 1) * 128].reshape(GB // SUB, SUB, 128)
                span = slice(n % 2 * 128, (n % 2 + 1) * 128)
                kept = n // 2 == (0 if left_gram else 1)
                target = keep_ref if kept else give_ref
                target[:, half, :, span] = tiles.astype(jnp.bfloat16)

    for left_gram in (True, False):
        for which in range(2):
            pl.when((col == (0 if left_gram else 1)) & (row == which))(
                functools.partial(emit, left_gram, which)
            )


def gram_pieces(place, quads):
    size = 2 * quads[0].shape[0]
    return pl.pallas_call(
        gram_kernel,
        in_specs=[whole(pltpu.SMEM)] + [whole()] * 4,
        out_specs=[whole()] * 4,
        out_shape=[
            jax.ShapeDtypeStruct((32, 2, SUB, WIDTH), jnp.bfloat16),
            jax.ShapeDtypeStruct((32, 2, SUB, WIDTH), jnp.bfloat16),
            jax.ShapeDtypeStruct((SUB, 128), jnp.bfloat16),
            pltpu.HBM((size, size), jnp.bfloat16),
        ],
        compiler_params=PARAMS,
        cost_estimate=pl.CostEstimate(
            flops=32 * 10**9, bytes_accessed=3 * 10**6, transcendentals=0
        ),
        name="gram_pieces",
    )(place, *quads)


GROUPS = 4


def second_kernel(
    facts_ref, rows_ref, keep_ref, other_ref, diagonal_ref, out_ref, live_ref, sems
):
    core = facts_ref[COL]
    items = live_ref.shape[0] // GROUPS
    pieces = []
    for n, source in enumerate((keep_ref, other_ref)):
        lane = pl.multiple_of(BASES + WIDTH * (core ^ n), WIDTH)
        pieces.append(
            pltpu.make_async_copy(
                source, out_ref.at[:, :, pl.ds(lane, WIDTH)], sems.at[GROUPS + n]
            )
        )
    owner = facts_ref[facts_ref[MINE]] // 4
    pieces.append(
        pltpu.make_async_copy(
            diagonal_ref, out_ref.at[owner, :, SPARE : SPARE + 128], sems.at[GROUPS + 2]
        )
    )
    for group in range(GROUPS):

        @pl.loop(items * group, items * (group + 1), unroll=True)
        def _(item, group=group):
            pltpu.make_async_copy(
                rows_ref.at[facts_ref[item]], live_ref.at[item], sems.at[group]
            ).start()

    for piece in pieces:
        piece.start()
    for group in range(GROUPS):
        pltpu.make_async_copy(
            rows_ref.at[0:items], live_ref.at[items * group : items * (group + 1)], sems.at[group]
        ).wait()

        @pl.loop(items // 2 * group, items // 2 * (group + 1), unroll=True)
        def _(block):
            left = live_ref[2 * block]
            right = live_ref[2 * block + 1]
            for i in range(2):
                at = (block // 4) * 8 + block % 4 + 4 * i
                out_ref[at, :, 0:512] = left[:, 512 * i : 512 * (i + 1)]
                out_ref[at, :, 512:BASES] = right

    for piece in pieces:
        piece.wait()


def second_operand(facts, rows, keep, other, diagonal):
    return pl.pallas_call(
        second_kernel,
        in_specs=[whole(pltpu.SMEM), whole(pl.ANY), whole(), whole(), whole()],
        out_specs=whole(),
        out_shape=pltpu.VMEM((CHIPS, SUB, SPARE + 128), jnp.bfloat16),
        scratch_shapes=[
            pltpu.VMEM((64, SUB, 1024), jnp.bfloat16),
            pltpu.SemaphoreType.DMA((GROUPS + 3,)),
        ],
        compiler_params=pltpu.CompilerParams(vmem_limit_bytes=8 * 2**20),
        cost_estimate=pl.CostEstimate(flops=0, bytes_accessed=8 * 10**6, transcendentals=0),
        name="second_operand",
    )(facts, rows, keep, other, diagonal)


def third_kernel(facts_ref, got_ref, out_ref, sems):
    @pl.loop(0, 32, unroll=True)
    def _(block):
        for side in range(2):
            code = facts_ref[2 * block + side]
            for half in range(2):
                source = (block // 4) * 8 + block % 4 + 4 * half
                lane = pl.multiple_of(code % 2 * (2 * WIDTH) + half * WIDTH, WIDTH)
                pltpu.make_async_copy(
                    got_ref.at[source, :, BASES + side * WIDTH : BASES + (side + 1) * WIDTH],
                    out_ref.at[code // 2, :, pl.ds(lane, WIDTH)],
                    sems.at[0],
                ).start()

    pltpu.make_async_copy(
        got_ref.at[:, :, BASES:SPARE], out_ref.at[0:CHIPS, :, 0 : 2 * WIDTH], sems.at[0]
    ).wait()


def third_operand(facts, got):
    return pl.pallas_call(
        third_kernel,
        in_specs=[whole(pltpu.SMEM), whole(pl.ANY)],
        out_specs=whole(pl.ANY),
        out_shape=pltpu.HBM((128, SUB, 4 * WIDTH), jnp.bfloat16),
        scratch_shapes=[pltpu.SemaphoreType.DMA((1,))],
        compiler_params=pltpu.CompilerParams(vmem_limit_bytes=8 * 2**20),
        cost_estimate=pl.CostEstimate(flops=0, bytes_accessed=4 * 10**6, transcendentals=0),
        name="third_operand",
    )(facts, pltpu.with_memory_space_constraint(got, pltpu.VMEM))


def rotate_kernel(
    facts_ref,
    block_ref,
    mine_ref,
    theirs_ref,
    first_ref,
    second_ref,
    new_first_ref,
    new_second_ref,
    direction_ref,
    spare_ref,
    held_ref,
    left_ref,
    right_ref,
    moment_ref,
    sems,
):
    col = facts_ref[COL]

    def load(source, target, n):
        return pltpu.make_async_copy(source, target, sems.at[n])

    def spare(source, n):
        item = facts_ref[NAMED + n // 2]
        block = item // 2
        chip = (block // 4 * 2 + n % 2) * 4 + block % 4
        return load(source.at[chip, :, SPARE : SPARE + 128], spare_ref.at[n], 16 + n)

    for n in range(4):
        same = facts_ref[NAMED + n // 2] % 2 == col
        pl.when(same)(spare(mine_ref, n).start)
        pl.when(jnp.logical_not(same))(spare(theirs_ref, n).start)

    lane = pl.multiple_of(512 + 512 * col, 512)
    lefts = []
    rights = []
    for n, source in enumerate((mine_ref, theirs_ref)):
        lefts.append(load(source.at[:, :, 0:512], left_ref.at[:, col ^ n], n))
        rights.append(load(source.at[:, :, pl.ds(lane, 512)], right_ref.at[:, col ^ n], 14 + n))
    for copy in lefts + rights:
        copy.start()
    load_block = load(block_ref, held_ref, 3)
    load_block.start()
    moments = [load(first_ref, moment_ref.at[0], 4), load(second_ref, moment_ref.at[1], 5)]
    for moment in moments:
        moment.start()
    for copy in lefts:
        copy.wait()
    load_block.wait()
    size = held_ref.shape[0]
    left_rot = dot_tn(left_ref[...].reshape(size, 512), held_ref[...]).astype(jnp.bfloat16)
    for copy in rights:
        copy.wait()
    for moment in moments:
        moment.wait()
    right = right_ref[...].reshape(size, 512)
    stores = []
    for part in range(4):
        rows = slice(128 * part, 128 * (part + 1))
        rotated = dot_nn(left_rot[rows], right)
        new_first = beta_one * moment_ref[0, rows] + (1.0 - beta_one) * rotated
        new_second = beta_two * moment_ref[1, rows] + (1.0 - beta_two) * rotated * rotated
        direction_ref[rows] = (new_first / (jnp.sqrt(new_second) + epsilon)).astype(jnp.bfloat16)
        moment_ref[0, rows] = new_first
        moment_ref[1, rows] = new_second
        for n, target in enumerate((new_first_ref, new_second_ref)):
            store = load(moment_ref.at[n, rows], target.at[rows], 6 + 2 * part + n)
            store.start()
            stores.append(store)
    for store in stores:
        store.wait()
    for n in range(4):
        spare(mine_ref, n).wait()


def rotate(facts, block, mine, theirs, first, second):
    half = first.shape[0]
    block, first, second = (
        pltpu.with_memory_space_constraint(value, pltpu.HBM) for value in (block, first, second)
    )
    return pl.pallas_call(
        rotate_kernel,
        in_specs=[whole(pltpu.SMEM)] + [whole(pl.ANY)] * 5,
        out_specs=[whole(pl.ANY), whole(pl.ANY), whole(), whole(pl.ANY)],
        out_shape=[
            jax.ShapeDtypeStruct((half, half), jnp.float32),
            jax.ShapeDtypeStruct((half, half), jnp.float32),
            jax.ShapeDtypeStruct((half, half), jnp.bfloat16),
            pltpu.HBM((4, SUB, 128), jnp.bfloat16),
        ],
        scratch_shapes=[
            pltpu.VMEM((1024, 1024), jnp.bfloat16),
            pltpu.VMEM((CHIPS, 2, SUB, 512), jnp.bfloat16),
            pltpu.VMEM((CHIPS, 2, SUB, 512), jnp.bfloat16),
            pltpu.VMEM((2, half, half), jnp.float32),
            pltpu.SemaphoreType.DMA((20,)),
        ],
        compiler_params=pltpu.CompilerParams(vmem_limit_bytes=20 * 2**20),
        cost_estimate=pl.CostEstimate(
            flops=16 * 10**8, bytes_accessed=10**7, transcendentals=10**6
        ),
        name="rotate",
    )(facts, block, mine, theirs, first, second)


def back_kernel(
    place_ref,
    own_ref,
    side_ref,
    mine_ref,
    theirs_ref,
    keep_ref,
    give_ref,
    left_ref,
    right_ref,
    strip_ref,
    sems,
):
    row = place_ref[0]
    col = place_ref[1]
    half = own_ref.shape[0]
    span = pl.ds(col * (CHIPS // 2), CHIPS // 2)
    lefts = []
    rights = []
    for n, source in enumerate((mine_ref, theirs_ref)):
        lefts.append(
            pltpu.make_async_copy(
                source.at[:, :, 0:512], left_ref.at[:, col ^ n], sems.at[n]
            )
        )
        rights.append(
            pltpu.make_async_copy(
                source.at[span, :, 512:BASES], right_ref.at[:, col ^ n], sems.at[2 + n]
            )
        )
    for copy in rights + lefts:
        copy.start()
    strip_ref[:, pl.ds(pl.multiple_of(col * half, half), half)] = own_ref[...]
    strip_ref[:, pl.ds(pl.multiple_of((1 - col) * half, half), half)] = side_ref[...]
    for copy in rights:
        copy.wait()
    half_back = dot_nt(strip_ref[...], right_ref[...].reshape(half, 1024)).astype(jnp.bfloat16)
    for copy in lefts:
        copy.wait()
    keep = left_ref[pl.ds(row * (CHIPS // 2), CHIPS // 2)].reshape(half, 512)
    give = left_ref[pl.ds((1 - row) * (CHIPS // 2), CHIPS // 2)].reshape(half, 512)
    give_ref[...] = dot_nn(give, half_back).astype(jnp.bfloat16)
    keep_ref[...] = dot_nn(keep, half_back)


def back(place, own, side, mine, theirs):
    half = own.shape[0]
    return pl.pallas_call(
        back_kernel,
        in_specs=[whole(pltpu.SMEM), whole(), whole(), whole(pl.ANY), whole(pl.ANY)],
        out_specs=[whole()] * 2,
        out_shape=[
            jax.ShapeDtypeStruct((half, half), jnp.float32),
            jax.ShapeDtypeStruct((half, half), jnp.bfloat16),
        ],
        scratch_shapes=[
            pltpu.VMEM((CHIPS, 2, SUB, 512), jnp.bfloat16),
            pltpu.VMEM((CHIPS // 2, 2, SUB, 1024), jnp.bfloat16),
            pltpu.VMEM((half, 2 * half), jnp.bfloat16),
            pltpu.SemaphoreType.DMA((4,)),
        ],
        compiler_params=PARAMS,
        cost_estimate=pl.CostEstimate(
            flops=11 * 10**8, bytes_accessed=6 * 10**6, transcendentals=0
        ),
        name="back",
    )(place, own, side, mine, theirs)


def finish_kernel(keep_ref, other_ref, out_ref, sum_ref, sems):
    parts = sems.shape[0]
    rows = sum_ref.shape[0] // parts
    stores = []
    for part in range(parts):
        span = slice(rows * part, rows * (part + 1))
        sum_ref[span] = keep_ref[span] + other_ref[span].astype(jnp.float32)
        stores.append(pltpu.make_async_copy(sum_ref.at[span], out_ref.at[span], sems.at[part]))
        stores[part].start()
    for store in stores:
        store.wait()


def finish(keep, other):
    keep, other = (
        pltpu.with_memory_space_constraint(value, pltpu.VMEM) for value in (keep, other)
    )
    return pl.pallas_call(
        finish_kernel,
        in_specs=[whole()] * 2,
        out_specs=whole(pl.ANY),
        out_shape=pltpu.HBM(keep.shape, keep.dtype),
        scratch_shapes=[
            pltpu.VMEM(keep.shape, keep.dtype),
            pltpu.SemaphoreType.DMA((4,)),
        ],
        compiler_params=pltpu.CompilerParams(vmem_limit_bytes=8 * 2**20),
        cost_estimate=pl.CostEstimate(
            flops=3 * 10**5, bytes_accessed=2 * 10**6, transcendentals=0
        ),
        name="finish",
    )(keep, other)


def settle_kernel(factor_ref, out_ref, ready_ref, strips_ref, sems):
    count = strips_ref.shape[0]
    loads = [
        pltpu.make_async_copy(factor_ref.at[strip_of(n)], strips_ref.at[n], sems.at[0, n])
        for n in range(count)
    ]
    stores = [
        pltpu.make_async_copy(strips_ref.at[n], out_ref.at[strip_of(n)], sems.at[1, n])
        for n in range(count)
    ]
    for load in loads:
        load.start()
    for n in range(count):
        loads[n].wait()
        stores[n].start()
        if n < READY:
            ready_ref[n] = shampoo_beta * strips_ref[n]
    for store in stores:
        store.wait()


def settle(factors):
    slots, size, _ = factors.shape
    return pl.pallas_call(
        settle_kernel,
        in_specs=[whole(pl.ANY)],
        out_specs=[whole(pl.ANY), whole()],
        out_shape=[
            pltpu.HBM(factors.shape, factors.dtype),
            pltpu.VMEM((READY, GB, size), factors.dtype),
        ],
        scratch_shapes=[
            pltpu.VMEM((4 * slots, GB, size), jnp.float32),
            pltpu.SemaphoreType.DMA((2, 4 * slots)),
        ],
        compiler_params=pltpu.CompilerParams(vmem_limit_bytes=12 * 2**20),
        cost_estimate=pl.CostEstimate(
            flops=0, bytes_accessed=16 * 10**6, transcendentals=0
        ),
        name="settle",
    )(pltpu.with_memory_space_constraint(factors, pltpu.HBM))


def strip_of(n):
    return (n // 4, slice(GB * (n % 4), GB * (n % 4 + 1)))


def factor_kernel(
    facts_ref,
    ready_ref,
    factor_ref,
    got_ref,
    spare_ref,
    out_ref,
    strips_ref,
    held_ref,
    diagonal_ref,
    sems,
):
    slots = factor_ref.shape[0]
    count = 4 * slots
    spans = [slice(2 * WIDTH * slot, 2 * WIDTH * (slot + 1)) for slot in range(slots)]
    pieces = [
        pltpu.make_async_copy(
            got_ref.at[:, :, :, span], held_ref.at[:, :, :, span], sems.at[2 * count + n]
        )
        for n, span in enumerate(spans)
    ]
    loads = {
        n: pltpu.make_async_copy(out_ref.at[strip_of(n)], strips_ref.at[n], sems.at[n])
        for n in range(READY, count)
    }
    stores = [
        pltpu.make_async_copy(strips_ref.at[n], out_ref.at[strip_of(n)], sems.at[count + n])
        for n in range(count)
    ]
    diagonals = pltpu.make_async_copy(spare_ref, diagonal_ref, sems.at[9 * slots])
    diagonals.start()
    for slot in range(slots):

        @pl.when(facts_ref[LIVE + slot] != 0)
        def _(slot=slot):
            pieces[slot].start()
            for n in range(max(READY, 4 * slot), 4 * (slot + 1)):
                loads[n].start()

    def piece(slot, which, n):
        lane = 2 * WIDTH * slot + (2 * which + n % 2) * 128
        halves = [
            held_ref[:, 2 * h + n // 2, :, lane : lane + 128]
            .astype(jnp.float32)
            .reshape(GB, 128)
            for h in range(2)
        ]
        return jnp.concatenate(halves, axis=1)

    def sub_block(slot, row, col):
        if row != col:
            pair = (min(row, col), max(row, col))
            which = 0 if pair in ABOVE[0] else 1
            value = piece(slot, which, ABOVE[which].index(pair))
            return value if row < col else value.T
        value = piece(slot, row // 2, 3)
        r, c = grid_positions()
        if row % 2 == 0:
            return jnp.where(r <= c, value, value.T)
        tile = diagonal_ref[2 * slot + row // 2].astype(jnp.float32)
        diagonal = jnp.concatenate([tile[0:1], tile[1:2]], axis=1)
        return jnp.where(r > c, value, jnp.where(r < c, value.T, diagonal))

    def mix(n):
        slot, row = n // 4, n % 4
        for col in range(4):
            span = slice(col * GB, (col + 1) * GB)
            if n < READY:
                decayed = ready_ref[n, :, span]
            else:
                decayed = shampoo_beta * strips_ref[n, :, span]
            strips_ref[n, :, span] = decayed + (1.0 - shampoo_beta) * sub_block(slot, row, col)

    diagonals.wait()
    for n in range(count):

        @pl.when(facts_ref[LIVE + n // 4] != 0)
        def _(n=n):
            if n % 4 == 0:
                pieces[n // 4].wait()
            if n >= READY:
                loads[n].wait()
            mix(n)
            stores[n].start()

    for n in range(count):
        pl.when(facts_ref[LIVE + n // 4] != 0)(stores[n].wait)


def update_factors(facts, ready, factors, got, spare):
    slots, size, _ = factors.shape
    got = got.reshape(32, 4, SUB, got.shape[2])
    return pl.pallas_call(
        factor_kernel,
        in_specs=[whole(pltpu.SMEM), whole()] + [whole(pl.ANY)] * 3,
        out_specs=whole(pl.ANY),
        out_shape=pltpu.HBM(factors.shape, factors.dtype),
        scratch_shapes=[
            pltpu.VMEM((4 * slots, GB, size), jnp.float32),
            pltpu.VMEM(got.shape, got.dtype),
            pltpu.VMEM(spare.shape, spare.dtype),
            pltpu.SemaphoreType.DMA((9 * slots + 1,)),
        ],
        input_output_aliases={2: 0},
        compiler_params=pltpu.CompilerParams(vmem_limit_bytes=20 * 2**20),
        cost_estimate=pl.CostEstimate(
            flops=4 * 10**6, bytes_accessed=2 * 10**7, transcendentals=0
        ),
        name="update_factors",
    )(
        facts,
        pltpu.with_memory_space_constraint(ready, pltpu.VMEM),
        pltpu.with_memory_space_constraint(factors, pltpu.HBM),
        got,
        spare,
    )


def shards(gradient, first_moment, second_moment, factors, eigen_bases, owners):
    devices = lax.axis_size("fsdp") * lax.axis_size("rep")
    slots = factors.shape[0]
    size = factors.shape[1]
    item_count = owners.shape[0]
    fsdp_index = lax.axis_index("fsdp")
    rep_index = lax.axis_index("rep")
    my_index = fsdp_index * lax.axis_size("rep") + rep_index
    my_item = (fsdp_index // 2 * 8 + rep_index).reshape(1).astype(jnp.int32)
    place = jnp.stack([fsdp_index % 2, rep_index % 2]).astype(jnp.int32)

    below = swap_neighbour(gradient, "fsdp")
    first_parts = interleave(eigen_bases, devices)
    first_got = lax.all_to_all(first_parts, BOTH, 0, 0, tiled=True)

    item_index = jnp.arange(item_count, dtype=jnp.int32)
    earlier_same = (owners[:, None] == owners[None, :]) & (
        item_index[None, :] < item_index[:, None]
    )
    codes = slots * owners + jnp.sum(earlier_same.astype(jnp.int32), axis=1)
    my_codes = my_index * slots + jnp.arange(slots, dtype=jnp.int32)
    hits = (codes[None, :] == my_codes[:, None]).astype(jnp.int32)
    live = jnp.sum(hits, axis=1)
    items = jnp.sum(hits * item_index[None, :], axis=1)
    facts = jnp.concatenate([codes, place, my_item, live, items]).astype(jnp.int32)

    side = swap_neighbour(gradient, "rep")
    cross = swap_neighbour(below, "rep")
    quads = (gradient, side, below, cross)
    settled, ready = settle(factors)
    kept_gram, given_gram, diagonal, block = gram_pieces(place, quads)
    other_gram = swap_neighbour(given_gram.reshape(CHIPS, SUB, WIDTH), "rep")
    kept_gram = kept_gram.reshape(CHIPS, SUB, WIDTH)

    second_parts = second_operand(
        facts, first_got.reshape(devices * slots, SUB, size), kept_gram, other_gram, diagonal
    )
    same_core = [[2 * chip + core for chip in range(CHIPS)] for core in range(2)]
    mine = lax.all_to_all(
        second_parts, BOTH, 0, 0, axis_index_groups=same_core, tiled=True
    )
    theirs = swap_neighbour(mine, "rep")

    third_parts = third_operand(facts, mine)
    third_got = lax.all_to_all(third_parts, BOTH, 0, 0, tiled=True)

    new_first, new_second, direction, spare = rotate(
        facts, block, mine, theirs, first_moment, second_moment
    )
    other = swap_neighbour(direction, "rep")
    keep, give = back(place, direction, other, mine, theirs)
    update = finish(keep, swap_neighbour(give, "fsdp"))
    new_factors = update_factors(facts, ready, settled, third_got, spare)
    return (update, new_first, new_second, new_factors)


def solution(mesh):
    in_specs = (
        P("fsdp", "rep"),
        P("fsdp", "rep"),
        P("fsdp", "rep"),
        P(("fsdp", "rep"), None, None),
        P(("fsdp", "rep"), None, None),
        P(),
    )
    out_specs = (
        P("fsdp", "rep"),
        P("fsdp", "rep"),
        P("fsdp", "rep"),
        P(("fsdp", "rep"), None, None),
    )
    return jax.shard_map(shards, mesh=mesh, in_specs=in_specs, out_specs=out_specs, check_vma=False)
```
